512 devices in a mesh: queue: 64 (over z_hi, y, core), seq: 8 (over x, z_lo).
Axes of the slice: x: 4, y: 8, z: 8 (z_hi: 4, z_lo: 2; z = z_hi * 2 + z_lo), core: 2. Of those that a mesh axis runs over, the one named last changes fastest.
Arguments:
- queries: bfloat16 [64, 1024, 3072], P('queue', 'seq'), may hold values from -18 to 18
- key_proj: bfloat16 [64, 1024, 3072], P('queue', 'seq'), may hold values from -18 to 18
- values: bfloat16 [64, 1024, 3072], P('queue', 'seq'), may hold values from -6 to 6
- latents: float32 [64, 1024, 64], P('queue', 'seq'), may hold values from -6 to 6
- head_weight: bfloat16 [3072, 64], replicated, may hold values from -0.109375 to 0.109375
- levels: int32 [64], P('queue'), may hold values from 1 to 256, as said below
- timesteps: int32 [257], replicated, may hold values from 0 to 10240, as said below
- fresh_noise: float32 [1024, 64], P('seq'), may hold values from -6 to 6
Outputs:
- next_queue: float32 [64, 1024, 64], P('queue', 'seq')
- velocity: float32 [64, 1024, 64], P('queue', 'seq')
The draws below stay inside these ranges and needn't reach their ends.
Inputs may be any that keep to these rules, and one draw needn't show every extreme that they name: `levels`: strictly rising along the queue; position f holds a value from 4 f + 1 to 4 f + 4; the first position holds 1 and the last 256. `timesteps`: strictly rising, starting at 0, with steps of 16 to 64; the steps into levels 2 k + 1 and 2 k + 2 sum to 80.
All inputs are finite; a program needn't handle non-finite values.
Results may differ from the reference program's by a relative error of at most 0.0033.
Values may be sent and summed in bfloat16 or wider, within the bound.
No kernel may reach another device: no remote copies, remote signals or barrier semaphores. Data moves between devices by JAX's collectives and lax.ppermute only.
A program may use at most 64 MiB of HBM per device.

```python
import jax
import jax.numpy as jnp
from jax import lax

HEADS = 24
HS = 128
PATCH = 64
FRAMES = 64
TOKENS = 1024
LEVELS = 257


def draw_queries(key, part):
    key = jax.random.fold_in(key, 11)
    drawn = jnp.clip(2.5 * jax.random.normal(key, (FRAMES, TOKENS, HEADS * HS), jnp.float32), -12.0, 12.0)
    return drawn.astype(jnp.bfloat16)


def draw_key_proj(key, part):
    key = jax.random.fold_in(key, 12)
    drawn = jnp.clip(jax.random.normal(key, (FRAMES, TOKENS, HEADS * HS), jnp.float32), -6.0, 6.0)
    return drawn.astype(jnp.bfloat16)


def draw_levels(key, part):
    key = jax.random.fold_in(key, 13)
    offset = jax.random.randint(key, (FRAMES,), 0, 4, jnp.int32)
    offset = offset.at[0].set(0).at[FRAMES - 1].set(3)
    return (4 * jnp.arange(FRAMES, dtype=jnp.int32) + 1 + offset).astype(jnp.int32)


def draw_timesteps(key, part):
    key = jax.random.fold_in(key, 14)
    first = jax.random.randint(key, ((LEVELS - 1) // 2,), 16, 65, jnp.int32)
    increments = jnp.stack([first, 80 - first], axis=1).reshape(-1).astype(jnp.int32)
    return jnp.concatenate([jnp.zeros((1,), jnp.int32), jnp.cumsum(increments).astype(jnp.int32)])


def block_levels(own_key, shape, split, smallest, high):
    def one(dim, shards_of):
        steps = jax.random.uniform(jax.random.fold_in(jax.random.fold_in(own_key, 6), dim), (shards_of,), jnp.float32, smallest / len(split), high / len(split))
        return jnp.repeat(jnp.exp(steps), shape[dim] // shards_of).reshape((-1,) + (1,) * (len(shape) - dim - 1))

    level = one(*split[0])
    for cut in split[1:]:
        level = level * one(*cut)
    return level


def gaussian(own_key, dims, scale, bound, shards=(), kind=jnp.bfloat16):
    entries = jax.random.normal(own_key, dims, jnp.float32) * scale
    if len(shards) > 0:
        entries = block_levels(own_key, dims, shards, -0.22, 0.18) * entries
    return jnp.clip(entries, min=-bound, max=bound).astype(kind)


def setup_inputs(seed: int = 0) -> dict:
    streams_of = jax.random.split(jax.random.key(seed), 9)
    queries = draw_queries(jax.random.fold_in(streams_of[8], 71), 0)
    key_proj = draw_key_proj(jax.random.fold_in(streams_of[8], 71), 0)
    values = gaussian(streams_of[2], (FRAMES, TOKENS, HEADS * HS), 1.0, 6.0, ((0, 64), (1, 8)))
    latents = gaussian(streams_of[3], (FRAMES, TOKENS, PATCH), 1.0, 6.0, ((0, 64), (1, 8)), jnp.float32)
    head_weight = gaussian(streams_of[4], (HEADS * HS, PATCH), (HEADS * HS) ** -0.5, 0.109375)
    levels = draw_levels(jax.random.fold_in(streams_of[8], 71), 0)
    timesteps = draw_timesteps(jax.random.fold_in(streams_of[8], 71), 0)
    fresh_noise = gaussian(streams_of[7], (TOKENS, PATCH), 1.0, 6.0, ((0, 8),), jnp.float32)
    return dict(queries=queries, key_proj=key_proj, values=values, latents=latents, head_weight=head_weight, levels=levels, timesteps=timesteps, fresh_noise=fresh_noise)


def reference(queries, key_proj, values, latents, head_weight, levels, timesteps, fresh_noise):
    scale = HS ** -0.5
    frames, tokens, width = queries.shape
    zero_frame = jnp.zeros((1, tokens, width), jnp.bfloat16)
    key_padded = jnp.concatenate([zero_frame, key_proj, zero_frame], axis=0)
    value_padded = jnp.concatenate([zero_frame, values, zero_frame], axis=0)

    def one_frame(frame):
        query_rows = lax.dynamic_slice_in_dim(queries, frame, 1, 0)[0].reshape(tokens, HEADS, HS).astype(jnp.float32)
        key_rows = lax.dynamic_slice_in_dim(key_padded, frame, 3, 0).reshape(3 * tokens, HEADS, HS).astype(jnp.float32)
        value_rows = lax.dynamic_slice_in_dim(value_padded, frame, 3, 0).reshape(3 * tokens, HEADS, HS).astype(jnp.float32)
        neighbour = frame - 1 + jnp.arange(3, dtype=jnp.int32)
        frame_ok = (neighbour >= 0) & (neighbour < frames)
        key_ok = jnp.repeat(frame_ok, tokens)
        scores = jnp.einsum("qhd,khd->hqk", query_rows, key_rows) * scale
        scores = jnp.where(key_ok[None, None, :], scores, -jnp.inf)
        row_peak = jnp.max(scores, axis=2, keepdims=True)
        weights = jnp.exp(scores - row_peak)
        totals = jnp.sum(weights, axis=2)
        rounded = lax.optimization_barrier(weights.astype(jnp.bfloat16)).astype(jnp.float32)
        mixed = jnp.einsum("hqk,khd->qhd", rounded, value_rows) / totals.T[:, :, None]
        attended = mixed.astype(jnp.bfloat16).reshape(tokens, HEADS * HS)
        return jnp.dot(attended, head_weight, preferred_element_type=jnp.float32)

    velocity = lax.map(one_frame, jnp.arange(frames, dtype=jnp.int32))
    time_now = timesteps[levels]
    time_before = timesteps[jnp.maximum(levels - 2, 0).astype(jnp.int32)]
    step_size = (time_before - time_now).astype(jnp.float32) / 64.0
    advanced = latents + step_size[:, None, None] * velocity
    next_queue = jnp.concatenate([advanced[1:], fresh_noise[None]], axis=0)
    return next_queue, velocity
```

```python
import math

import jax
import jax.numpy as jnp
from jax import lax
from jax.experimental import pallas as pl
from jax.experimental.pallas import tpu as pltpu
from jax.sharding import PartitionSpec as P

HS = 128
HALF = 64
MIB = 1 << 20
NT = (((1,), (1,)), ((), ()))
VMEM = pl.BlockSpec(memory_space=pltpu.VMEM)
SMEM = pl.BlockSpec(memory_space=pltpu.SMEM)


def pack_kv_kernel(key_ref, value_ref, weight_ref, out_ref):
    tokens = key_ref.shape[0]
    for h in range(3):
        out_ref[0, h * tokens : (h + 1) * tokens, :] = key_ref[:, h * HS : (h + 1) * HS]
    weight = [weight_ref[:, h * HS : (h + 1) * HS] for h in range(3)]
    zero = jnp.zeros_like(weight[0])

    def diagonal(a, b):
        return jnp.concatenate(
            [jnp.concatenate([a, zero], axis=1), jnp.concatenate([zero, b], axis=1)], axis=0
        )

    half = tokens // 2
    first = lax.dot_general(
        value_ref[:, : 2 * HS], diagonal(weight[0], weight[1]), NT, preferred_element_type=jnp.float32
    )
    third = jnp.concatenate([value_ref[:half, 2 * HS :], value_ref[half:, 2 * HS :]], axis=1)
    third = lax.dot_general(
        third, diagonal(weight[2], weight[2]), NT, preferred_element_type=jnp.float32
    )
    out_ref[0, 3 * tokens : 4 * tokens, :] = first.astype(jnp.bfloat16)
    out_ref[0, 4 * tokens :, :] = third.astype(jnp.bfloat16)


def pack_kv(keys, values, weight_t, groups):
    tokens, width = keys.shape
    part = width // groups
    rows = tokens * 3 + tokens + tokens // 2
    return pl.pallas_call(
        pack_kv_kernel,
        grid=(groups,),
        in_specs=[
            pl.BlockSpec((tokens, part), lambda s: (0, s)),
            pl.BlockSpec((tokens, part), lambda s: (0, s)),
            pl.BlockSpec((HALF, part), lambda s: (0, s)),
        ],
        out_specs=pl.BlockSpec((1, rows, HS), lambda s: (s, 0, 0)),
        out_shape=jax.ShapeDtypeStruct((groups, rows, HS), jnp.bfloat16),
        name="pack_kv",
    )(keys, values, weight_t)


def pack_q_kernel(query_ref, out_ref):
    tokens = query_ref.shape[0]
    for h in range(3):
        out_ref[0, h * tokens : (h + 1) * tokens, :] = query_ref[:, h * HS : (h + 1) * HS]


def pack_q(queries, groups):
    tokens, width = queries.shape
    part = width // groups
    return pl.pallas_call(
        pack_q_kernel,
        grid=(groups,),
        in_specs=[pl.BlockSpec((tokens, part), lambda s: (0, s))],
        out_specs=pl.BlockSpec((1, 3 * tokens, HS), lambda s: (s, 0, 0)),
        out_shape=jax.ShapeDtypeStruct((groups, 3 * tokens, HS), jnp.bfloat16),
        name="pack_q",
    )(queries)


def scaled_queries(query_ref, split_ref):
    groups, rows, _ = query_ref.shape
    tokens = rows // 3
    scale = HS ** (-0.5) * math.log2(math.e)
    for h in range(3):
        q = query_ref[:, h * tokens : (h + 1) * tokens, :].reshape(groups * tokens, HS)
        q = q.astype(jnp.float32) * scale
        high = q.astype(jnp.bfloat16)
        low = (q - high.astype(jnp.float32)).astype(jnp.bfloat16)
        split_ref[h, :, :HS] = high
        split_ref[h, :, HS:] = low


def attend(split_ref, kv_ref, block_rows, emit):
    groups, rows, _ = kv_ref.shape
    tokens = rows * 2 // 9
    count = groups * tokens
    pair = kv_ref[:, 3 * tokens : 4 * tokens, :].reshape(count, HS)
    last = kv_ref[:, 4 * tokens :, :]
    swapped = jnp.concatenate([last[:, :, HALF:], last[:, :, :HALF]], axis=2)
    last = jnp.concatenate([last, swapped], axis=1).reshape(count, HS)
    ones = jnp.ones((count, HS), jnp.bfloat16)
    for h in range(3):
        k = kv_ref[:, h * tokens : (h + 1) * tokens, :].reshape(count, HS)
        keys = jnp.concatenate([k, k], axis=1)
        mix = jnp.concatenate([last if h == 2 else pair, ones], axis=1)
        for b in range(count // block_rows):
            span = slice(b * block_rows, (b + 1) * block_rows)
            scores = lax.dot_general(split_ref[h, span, :], keys, NT, preferred_element_type=jnp.float32)
            peak = jnp.ceil(jnp.max(scores, axis=1, keepdims=True))
            probs = jnp.exp2(scores - peak).astype(jnp.bfloat16)
            emit(h, span, peak, jnp.dot(probs, mix, preferred_element_type=jnp.float32))


def lanes(h, rows):
    lane = lax.broadcasted_iota(jnp.int32, (rows, HS), 1)
    if h == 1:
        lane = HS - 1 - lane
    return lane


def packed(h, peak, mixed):
    lane = lanes(h, mixed.shape[0])
    return jnp.where(lane < HALF, mixed[:, :HS], jnp.where(lane < HALF + 32, mixed[:, HS:], peak))


def unpacked(h, state):
    total, peak = (HALF, HALF + 32) if h != 1 else (HALF - 1, 0)
    return state[:, total : total + 1], state[:, peak : peak + 1]


def own_kernel(query_ref, kv_ref, state_ref, split_ref):
    scaled_queries(query_ref, split_ref)

    def emit(h, span, peak, mixed):
        state_ref[h, span, :] = packed(h, peak, mixed)

    attend(split_ref, kv_ref, 256, emit)


def halo_kernel(ok_ref, query_ref, before_ref, after_ref, own_ref, out_ref, split_ref, state_ref):
    scaled_queries(query_ref, split_ref)
    state_ref[...] = own_ref[...]

    def emit(h, span, peak, mixed):
        state = state_ref[h, span, :]
        _, old_peak = unpacked(h, state)
        new_peak = jnp.maximum(old_peak, peak)
        new = packed(h, new_peak, mixed)
        kept, added = jnp.exp2(old_peak - new_peak), jnp.exp2(peak - new_peak)
        lane = lanes(h, state.shape[0])
        state_ref[h, span, :] = jnp.where(lane < HALF + 32, state * kept + new * added, new)

    for i, ref in enumerate((before_ref, after_ref)):
        @pl.when(ok_ref[i] > 0)
        def _():
            attend(split_ref, ref, 256, emit)

    groups, _, tokens = out_ref.shape
    for s in range(groups):
        span = slice(s * tokens, (s + 1) * tokens)
        parts = []
        for h in range(3):
            state = state_ref[h, span, :]
            total, _ = unpacked(h, state)
            parts.append(state / total)
        lane = lanes(0, tokens)
        both = jnp.where(lane < HALF, parts[0] + parts[2], parts[1])
        turned = both.T
        out_ref[s] = turned[:HALF] + turned[HALF:]


def params(mib):
    return pltpu.CompilerParams(vmem_limit_bytes=mib * MIB)


def attend_own(q, kv):
    count = q.shape[0] * q.shape[1] // 3
    return pl.pallas_call(
        own_kernel,
        in_specs=[VMEM] * 2,
        out_specs=VMEM,
        out_shape=jax.ShapeDtypeStruct((3, count, HS), jnp.float32),
        scratch_shapes=[pltpu.VMEM((3, count, 2 * HS), jnp.bfloat16)],
        compiler_params=params(24),
        cost_estimate=pl.CostEstimate(
            flops=12 * count * count * 256, bytes_accessed=8 * MIB, transcendentals=3 * count * count
        ),
        name="attend_own",
    )(q, kv)


def attend_halo(ok, q, before, after, own):
    groups, rows, _ = q.shape
    tokens = rows // 3
    count = groups * tokens
    return pl.pallas_call(
        halo_kernel,
        in_specs=[SMEM] + [VMEM] * 4,
        out_specs=VMEM,
        out_shape=jax.ShapeDtypeStruct((groups, HALF, tokens), jnp.float32),
        scratch_shapes=[
            pltpu.VMEM((3, count, 2 * HS), jnp.bfloat16),
            pltpu.VMEM((3, count, HS), jnp.float32),
        ],
        compiler_params=params(24),
        cost_estimate=pl.CostEstimate(
            flops=24 * count * count * 256, bytes_accessed=8 * MIB, transcendentals=6 * count * count
        ),
        name="attend_halo",
    )(ok, q, before, after, own)


def finish_kernel(position_ref, levels_ref, timesteps_ref, parts_ref, latent_ref, fresh_ref, velocity_ref, sent_ref):
    velocity = parts_ref[0]
    for s in range(1, parts_ref.shape[0]):
        velocity = velocity + parts_ref[s]
    level = levels_ref[0]
    step = timesteps_ref[jnp.maximum(level - 2, 0)] - timesteps_ref[level]
    velocity_ref[...] = velocity
    advanced = latent_ref[...] + (step.astype(jnp.float32) / 64.0) * velocity
    sent_ref[...] = jnp.where(position_ref[0] == 0, fresh_ref[...], advanced)


def finish(position, levels, timesteps, parts, latent_t, fresh_t):
    shape = jax.ShapeDtypeStruct(latent_t.shape, jnp.float32)
    return pl.pallas_call(
        finish_kernel,
        in_specs=[SMEM] * 3 + [VMEM] * 3,
        out_specs=[VMEM] * 2,
        out_shape=[shape, shape],
        name="finish",
    )(position, levels, timesteps, parts, latent_t, fresh_t)


def on_device(queries, key_proj, values, latents, head_weight, levels, timesteps, fresh_noise):
    position = lax.axis_index("queue")
    length = lax.axis_size("queue")
    groups = lax.axis_size("seq")
    kv = pack_kv(key_proj[0], values[0], head_weight.T, groups)
    kv = lax.all_to_all(kv, "seq", split_axis=0, concat_axis=0, tiled=True)
    q = pack_q(queries[0], groups)
    q = lax.all_to_all(q, "seq", split_axis=0, concat_axis=0, tiled=True)
    up = [(i, i + 1) for i in range(length - 1)]
    before = lax.ppermute(kv, "queue", up)
    after = lax.ppermute(kv, "queue", [(j, i) for i, j in up])
    own = attend_own(q, kv)
    ok = jnp.stack([position > 0, position < length - 1]).astype(jnp.int32)
    parts = attend_halo(ok, q, before, after, own)
    parts = lax.all_to_all(parts, "seq", split_axis=0, concat_axis=0, tiled=True)
    velocity, sent = finish(
        position[None].astype(jnp.int32), levels, timesteps, parts, latents[0].T, fresh_noise.T
    )
    shifted = lax.ppermute(sent, "queue", [(i, (i - 1) % length) for i in range(length)])
    return (shifted.T[None], velocity.T[None])


def solution(mesh):
    in_specs = (
        P("queue", "seq", None),
        P("queue", "seq", None),
        P("queue", "seq", None),
        P("queue", "seq", None),
        P(),
        P("queue"),
        P(),
        P("seq", None),
    )
    out_specs = (P("queue", "seq", None), P("queue", "seq", None))
    return jax.shard_map(
        on_device, mesh=mesh, in_specs=in_specs, out_specs=out_specs, check_vma=False
    )
```

```python
import math

import jax
import jax.numpy as jnp
from jax import lax
from jax.experimental import pallas as pl
from jax.experimental.pallas import tpu as pltpu
from jax.sharding import PartitionSpec as P

HS = 128
HALF = 64
MIB = 1 << 20
ROWS = 256
NT = (((1,), (1,)), ((), ()))
VMEM = pl.BlockSpec(memory_space=pltpu.VMEM)
HBM = pl.BlockSpec(memory_space=pltpu.HBM)
SMEM = pl.BlockSpec(memory_space=pltpu.SMEM)


def pack_kv_kernel(key_ref, value_ref, weight_ref, out_ref, value_buf, weight_buf, key_sem, value_sem, weight_sem):
    groups, rows, part = out_ref.shape
    tokens = rows * 2 // 3
    half = tokens // 2
    keys, values, weights = [], [], []
    for s in range(groups):
        span = pl.ds(s * part, part)
        values.append(pltpu.make_async_copy(value_ref.at[:, span], value_buf.at[s], value_sem.at[s]))
        weights.append(pltpu.make_async_copy(weight_ref.at[:, span], weight_buf.at[s], weight_sem.at[s]))
        keys.append(pltpu.make_async_copy(key_ref.at[:, span], out_ref.at[s, pl.ds(0, tokens)], key_sem.at[s]))
        values[s].start()
        weights[s].start()
    for s in range(groups):
        keys[s].start()
    zero = jnp.zeros((HALF, HS), jnp.bfloat16)

    def diagonal(x, y):
        return jnp.concatenate(
            [jnp.concatenate([x, zero], axis=1), jnp.concatenate([zero, y], axis=1)], axis=0
        )

    for s in range(groups):
        values[s].wait()
        weights[s].wait()
        weight = [weight_buf[s, :, h * HS : (h + 1) * HS] for h in range(3)]
        pair = lax.dot_general(
            value_buf[s, :, : 2 * HS],
            diagonal(weight[0], weight[1]),
            NT,
            preferred_element_type=jnp.float32,
        ).astype(jnp.bfloat16)
        last = jnp.concatenate([value_buf[s, :half, 2 * HS :], value_buf[s, half:, 2 * HS :]], axis=1)
        last = lax.dot_general(
            last, diagonal(weight[2], weight[2]), NT, preferred_element_type=jnp.float32
        ).astype(jnp.bfloat16)
        out_ref[s, tokens:, :HS] = pair[:half]
        out_ref[s, tokens:, HS : 2 * HS] = pair[half:]
        out_ref[s, tokens:, 2 * HS :] = last
    for s in range(groups):
        keys[s].wait()


def params(mib):
    return pltpu.CompilerParams(vmem_limit_bytes=mib * MIB)


def pack_kv(keys, values, weight_t, groups):
    tokens, width = keys.shape
    part = width // groups
    return pl.pallas_call(
        pack_kv_kernel,
        in_specs=[HBM] * 3,
        out_specs=VMEM,
        out_shape=jax.ShapeDtypeStruct((groups, tokens * 3 // 2, part), jnp.bfloat16),
        scratch_shapes=[
            pltpu.VMEM((groups, tokens, part), jnp.bfloat16),
            pltpu.VMEM((groups, HALF, part), jnp.bfloat16),
            pltpu.SemaphoreType.DMA((groups,)),
            pltpu.SemaphoreType.DMA((groups,)),
            pltpu.SemaphoreType.DMA((groups,)),
        ],
        compiler_params=params(8),
        name="pack_kv",
    )(keys, values, weight_t)


def pack_q_kernel(query_ref, out_ref, sem):
    groups, _, part = out_ref.shape
    copies = [
        pltpu.make_async_copy(query_ref.at[:, pl.ds(s * part, part)], out_ref.at[s], sem.at[s])
        for s in range(groups)
    ]
    for copy in copies:
        copy.start()
    for copy in copies:
        copy.wait()


def pack_q(queries, groups):
    tokens, width = queries.shape
    part = width // groups
    return pl.pallas_call(
        pack_q_kernel,
        in_specs=[HBM],
        out_specs=VMEM,
        out_shape=jax.ShapeDtypeStruct((groups, tokens, part), jnp.bfloat16),
        scratch_shapes=[pltpu.SemaphoreType.DMA((groups,))],
        compiler_params=params(4),
        name="pack_q",
    )(queries)


def scaled_queries(query_ref, split_ref):
    groups, tokens, _ = query_ref.shape
    scale = HS ** (-0.5) * math.log2(math.e)
    for h in range(3):
        q = query_ref[:, :, h * HS : (h + 1) * HS].reshape(groups * tokens, HS)
        q = q.astype(jnp.float32) * scale
        high = q.astype(jnp.bfloat16)
        low = (q - high.astype(jnp.float32)).astype(jnp.bfloat16)
        split_ref[h, :, :HS] = high
        split_ref[h, :, HS:] = low


def attend(split_ref, kv_ref, emit):
    groups, rows, _ = kv_ref.shape
    tokens = rows * 2 // 3
    count = groups * tokens
    pair = [kv_ref[:, tokens:, :HS], kv_ref[:, tokens:, HS : 2 * HS]]
    pair = jnp.concatenate(pair, axis=1).reshape(count, HS)
    last = kv_ref[:, tokens:, 2 * HS :]
    swapped = jnp.concatenate([last[:, :, HALF:], last[:, :, :HALF]], axis=2)
    last = jnp.concatenate([last, swapped], axis=1).reshape(count, HS)
    ones = jnp.ones((count, HS), jnp.bfloat16)
    for h in range(3):
        k = kv_ref[:, :tokens, h * HS : (h + 1) * HS].reshape(count, HS)
        keys = jnp.concatenate([k, k], axis=1)
        mix = jnp.concatenate([last if h == 2 else pair, ones], axis=1)
        for b in range(split_ref.shape[1] // ROWS):
            span = slice(b * ROWS, (b + 1) * ROWS)
            scores = lax.dot_general(split_ref[h, span, :], keys, NT, preferred_element_type=jnp.float32)
            peak = jnp.ceil(jnp.max(scores, axis=1, keepdims=True))
            probs = jnp.exp2(scores - peak).astype(jnp.bfloat16)
            emit(h, span, peak, jnp.dot(probs, mix, preferred_element_type=jnp.float32))


def lanes(h, rows):
    lane = lax.broadcasted_iota(jnp.int32, (rows, HS), 1)
    if h == 1:
        lane = HS - 1 - lane
    return lane


def packed(h, peak, mixed):
    lane = lanes(h, mixed.shape[0])
    return jnp.where(lane < HALF, mixed[:, :HS], jnp.where(lane < HALF + 32, mixed[:, HS:], peak))


def unpacked(h, state):
    total, peak = (HALF, HALF + 32) if h != 1 else (HALF - 1, 0)
    return state[:, total : total + 1], state[:, peak : peak + 1]


def merge_into(state_ref):
    def emit(h, span, peak, mixed):
        state = state_ref[h, span, :]
        _, old_peak = unpacked(h, state)
        new_peak = jnp.maximum(old_peak, peak)
        new = packed(h, new_peak, mixed)
        kept, added = jnp.exp2(old_peak - new_peak), jnp.exp2(peak - new_peak)
        lane = lanes(h, state.shape[0])
        state_ref[h, span, :] = jnp.where(lane < HALF + 32, state * kept + new * added, new)

    return emit


def own_kernel(query_ref, kv_ref, state_ref, split_ref):
    scaled_queries(query_ref, split_ref)

    def emit(h, span, peak, mixed):
        state_ref[h, span, :] = packed(h, peak, mixed)

    attend(split_ref, kv_ref, emit)


def near_kernel(ok_ref, split_ref, before_ref, after_ref, own_ref, state_ref):
    state_ref[...] = own_ref[...]
    for i, ref in enumerate((before_ref, after_ref)):
        @pl.when(ok_ref[i] > 0)
        def _():
            attend(split_ref, ref, merge_into(state_ref))


def far_kernel(ok_ref, split_ref, direct_ref, turned_ref, near_ref, out_ref, state_ref, kv_ref):
    state_ref[...] = near_ref[...]

    @pl.when(ok_ref[2] > 0)
    def _():
        cut = direct_ref.shape[0]
        kv_ref[:cut] = direct_ref[...]
        kv_ref[cut:] = turned_ref[...]
        attend(split_ref, kv_ref, merge_into(state_ref))

    groups, _, tokens = out_ref.shape
    for s in range(groups):
        span = slice(s * tokens, (s + 1) * tokens)
        parts = []
        for h in range(3):
            state = state_ref[h, span, :]
            total, _ = unpacked(h, state)
            parts.append(state / total)
        lane = lanes(0, tokens)
        both = jnp.where(lane < HALF, parts[0] + parts[2], parts[1])
        turned = both.T
        out_ref[s] = turned[:HALF] + turned[HALF:]


def cost(frames, count):
    return pl.CostEstimate(
        flops=frames * 12 * count * count * 256,
        bytes_accessed=4 * MIB,
        transcendentals=frames * 3 * count * count,
    )


def attend_own(q, kv):
    count = q.shape[0] * q.shape[1]
    return pl.pallas_call(
        own_kernel,
        in_specs=[VMEM] * 2,
        out_specs=[VMEM] * 2,
        out_shape=[
            jax.ShapeDtypeStruct((3, count, HS), jnp.float32),
            jax.ShapeDtypeStruct((3, count, 2 * HS), jnp.bfloat16),
        ],
        compiler_params=params(16),
        cost_estimate=cost(1, count),
        name="attend_own",
    )(q, kv)


def attend_near(ok, split, before, after, state):
    return pl.pallas_call(
        near_kernel,
        in_specs=[SMEM] + [VMEM] * 4,
        out_specs=VMEM,
        out_shape=jax.ShapeDtypeStruct(state.shape, jnp.float32),
        compiler_params=params(16),
        cost_estimate=cost(2, state.shape[1]),
        name="attend_near",
    )(ok, split, before, after, state)


def attend_far(ok, split, direct, turned, state, groups):
    count = state.shape[1]
    whole = (direct.shape[0] + turned.shape[0],) + direct.shape[1:]
    return pl.pallas_call(
        far_kernel,
        in_specs=[SMEM] + [VMEM] * 4,
        out_specs=VMEM,
        out_shape=jax.ShapeDtypeStruct((groups, HALF, count // groups), jnp.float32),
        scratch_shapes=[pltpu.VMEM(state.shape, jnp.float32), pltpu.VMEM(whole, jnp.bfloat16)],
        compiler_params=params(16),
        cost_estimate=cost(1, count),
        name="attend_far",
    )(ok, split, direct, turned, state)


def finish_kernel(position_ref, levels_ref, timesteps_ref, parts_ref, latent_ref, fresh_ref, velocity_ref, sent_ref):
    velocity = parts_ref[0]
    for s in range(1, parts_ref.shape[0]):
        velocity = velocity + parts_ref[s]
    level = levels_ref[0]
    step = timesteps_ref[jnp.maximum(level - 2, 0)] - timesteps_ref[level]
    velocity_ref[...] = velocity
    advanced = latent_ref[...] + (step.astype(jnp.float32) / 64.0) * velocity
    sent_ref[...] = jnp.where(position_ref[0] == 0, fresh_ref[...], advanced)


def finish(position, levels, timesteps, parts, latent_t, fresh_t):
    shape = jax.ShapeDtypeStruct(latent_t.shape, jnp.float32)
    return pl.pallas_call(
        finish_kernel,
        in_specs=[SMEM] * 3 + [VMEM] * 3,
        out_specs=[VMEM] * 2,
        out_shape=[shape, shape],
        compiler_params=params(2),
        name="finish",
    )(position, levels, timesteps, parts, latent_t, fresh_t)


def turned(pairs):
    return [(j, i) for i, j in pairs]


def on_device(queries, key_proj, values, latents, head_weight, levels, timesteps, fresh_noise):
    position = lax.axis_index("queue")
    length = lax.axis_size("queue")
    groups = lax.axis_size("seq")
    kv = pack_kv(key_proj[0], values[0], head_weight.T, groups)
    kv = lax.all_to_all(kv, "seq", split_axis=0, concat_axis=0, tiled=True)
    q = pack_q(queries[0], groups)
    q = lax.all_to_all(q, "seq", split_axis=0, concat_axis=0, tiled=True)
    column = length // 4
    up = [(i, i + 1) for i in range(length - 1) if (i + 1) % column]
    before = lax.ppermute(kv, "queue", up)
    after = lax.ppermute(kv, "queue", turned(up))
    cross = [(i, i + 1) for i in range(column - 1, length - 1, column)]
    along_z = [(i, i + column) for i, _ in cross] + [(j, j - column) for _, j in cross]
    along_y = [(i + column, j) for i, j in cross] + [(j - column, i) for i, j in cross]
    cut = groups * 5 // 8
    direct = lax.ppermute(kv[:cut], "queue", cross + turned(cross))
    carried = lax.ppermute(kv[cut:], "queue", along_z)
    carried = lax.ppermute(carried, "queue", along_y)
    place = position % column
    has_before, has_after = place > 0, place < column - 1
    has_far = ((place == 0) & (position > 0)) | ((place == column - 1) & (position < length - 1))
    ok = jnp.stack([has_before, has_after, has_far]).astype(jnp.int32)
    state, split = attend_own(q, kv)
    state = attend_near(ok, split, before, after, state)
    parts = attend_far(ok, split, direct, carried, state, groups)
    parts = lax.all_to_all(parts, "seq", split_axis=0, concat_axis=0, tiled=True)
    velocity, sent = finish(
        position[None].astype(jnp.int32), levels, timesteps, parts, latents[0].T, fresh_noise.T
    )
    shifted = lax.ppermute(sent, "queue", [(i, (i - 1) % length) for i in range(length)])
    return (shifted.T[None], velocity.T[None])


def solution(mesh):
    in_specs = (
        P("queue", "seq", None),
        P("queue", "seq", None),
        P("queue", "seq", None),
        P("queue", "seq", None),
        P(),
        P("queue"),
        P(),
        P("seq", None),
    )
    out_specs = (P("queue", "seq", None), P("queue", "seq", None))
    return jax.shard_map(
        on_device, mesh=mesh, in_specs=in_specs, out_specs=out_specs, check_vma=False
    )
```

```python
import math

import jax
import jax.numpy as jnp
from jax import lax
from jax.experimental import pallas as pl
from jax.experimental.pallas import tpu as pltpu
from jax.sharding import PartitionSpec as P

HS = 128
HALF = 64
MIB = 1 << 20
ROWS = 256
PACK_MIB = 56
CUT = 5
NT = (((1,), (1,)), ((), ()))
VMEM = pl.BlockSpec(memory_space=pltpu.VMEM)
HBM = pl.BlockSpec(memory_space=pltpu.HBM)
SMEM = pl.BlockSpec(memory_space=pltpu.SMEM)


def pack_kernel(query_ref, key_ref, value_ref, weight_ref, out_ref, value_buf, weight_buf, query_sem, key_sem, value_sem, weight_sem):
    groups, rows, part = out_ref.shape
    tokens = rows * 2 // 5
    half = tokens // 2
    queries, keys, values, weights = [], [], [], []
    for s in range(groups):
        span = pl.ds(s * part, part)
        values.append(pltpu.make_async_copy(value_ref.at[:, span], value_buf.at[s], value_sem.at[s]))
        weights.append(pltpu.make_async_copy(weight_ref.at[:, span], weight_buf.at[s], weight_sem.at[s]))
        keys.append(pltpu.make_async_copy(key_ref.at[:, span], out_ref.at[s, pl.ds(tokens, tokens)], key_sem.at[s]))
        queries.append(pltpu.make_async_copy(query_ref.at[:, span], out_ref.at[s, pl.ds(0, tokens)], query_sem.at[s]))
        values[s].start()
        weights[s].start()
    for s in range(groups):
        queries[s].start()
        keys[s].start()
    zero = jnp.zeros((HALF, HS), jnp.bfloat16)

    def diagonal(x, y):
        return jnp.concatenate(
            [jnp.concatenate([x, zero], axis=1), jnp.concatenate([zero, y], axis=1)], axis=0
        )

    for s in range(groups):
        values[s].wait()
        weights[s].wait()
        weight = [weight_buf[s, :, h * HS : (h + 1) * HS] for h in range(3)]
        pair = lax.dot_general(
            value_buf[s, :, : 2 * HS],
            diagonal(weight[0], weight[1]),
            NT,
            preferred_element_type=jnp.float32,
        ).astype(jnp.bfloat16)
        last = jnp.concatenate([value_buf[s, :half, 2 * HS :], value_buf[s, half:, 2 * HS :]], axis=1)
        last = lax.dot_general(
            last, diagonal(weight[2], weight[2]), NT, preferred_element_type=jnp.float32
        ).astype(jnp.bfloat16)
        out_ref[s, 2 * tokens :, :HS] = pair[:half]
        out_ref[s, 2 * tokens :, HS : 2 * HS] = pair[half:]
        out_ref[s, 2 * tokens :, 2 * HS :] = last
    for s in range(groups):
        queries[s].wait()
        keys[s].wait()


def params(mib):
    return pltpu.CompilerParams(vmem_limit_bytes=mib * MIB)


def pack(queries, keys, values, weight_t, groups):
    tokens, width = keys.shape
    part = width // groups
    return pl.pallas_call(
        pack_kernel,
        in_specs=[HBM] * 4,
        out_specs=VMEM,
        out_shape=jax.ShapeDtypeStruct((groups, tokens * 5 // 2, part), jnp.bfloat16),
        scratch_shapes=[
            pltpu.VMEM((groups, tokens, part), jnp.bfloat16),
            pltpu.VMEM((groups, HALF, part), jnp.bfloat16),
        ]
        + [pltpu.SemaphoreType.DMA((groups,))] * 4,
        compiler_params=params(PACK_MIB),
        name="pack",
    )(queries, keys, values, weight_t)


def scaled_queries(query_ref, split_ref):
    groups, rows, _ = query_ref.shape
    tokens = rows * 2 // 5
    scale = HS ** (-0.5) * math.log2(math.e)
    for h in range(3):
        q = query_ref[:, :tokens, h * HS : (h + 1) * HS].reshape(groups * tokens, HS)
        q = q.astype(jnp.float32) * scale
        high = q.astype(jnp.bfloat16)
        low = (q - high.astype(jnp.float32)).astype(jnp.bfloat16)
        split_ref[h, :, :HS] = high
        split_ref[h, :, HS:] = low


def keys_and_values(ref, tokens, start, h):
    groups = ref.shape[0]
    count = groups * tokens
    k = ref[:, start : start + tokens, h * HS : (h + 1) * HS].reshape(count, HS)
    start += tokens
    if h == 2:
        first = ref[:, start : start + tokens // 2, 2 * HS :]
        second = jnp.concatenate([first[:, :, HALF:], first[:, :, :HALF]], axis=2)
    else:
        first = ref[:, start : start + tokens // 2, :HS]
        second = ref[:, start : start + tokens // 2, HS : 2 * HS]
    mix = jnp.concatenate([first, second], axis=1).reshape(count, HS)
    return k, mix


def attend(split_ref, sources, emit):
    for h in range(3):
        parts = [keys_and_values(ref, tokens, start, h) for ref, tokens, start in sources]
        k = jnp.concatenate([part[0] for part in parts], axis=0)
        mix = jnp.concatenate([part[1] for part in parts], axis=0)
        k = jnp.concatenate([k, k], axis=1)
        mix = jnp.concatenate([mix, jnp.ones_like(mix)], axis=1)
        for b in range(split_ref.shape[1] // ROWS):
            span = slice(b * ROWS, (b + 1) * ROWS)
            scores = lax.dot_general(split_ref[h, span, :], k, NT, preferred_element_type=jnp.float32)
            peak = jnp.ceil(jnp.max(scores, axis=1, keepdims=True))
            probs = jnp.exp2(scores - peak).astype(jnp.bfloat16)
            emit(h, span, peak, jnp.dot(probs, mix, preferred_element_type=jnp.float32))


def near_kernel(own_ref, mate_ref, sums_ref, totals_ref, peaks_ref, split_ref):
    scaled_queries(own_ref, split_ref)
    tokens = own_ref.shape[1] * 2 // 5

    def emit(h, span, peak, mixed):
        sums_ref[h, span, :] = mixed[:, :HS]
        totals_ref[h, span, :] = mixed[:, HS:]
        peaks_ref[h, span, :] = jnp.broadcast_to(peak, (ROWS, HS))

    attend(split_ref, [(own_ref, tokens, tokens), (mate_ref, tokens, tokens)], emit)


def far_kernel(flag_ref, split_ref, direct_ref, plain_ref, carried_ref, sums_ref, totals_ref, peaks_ref, out_ref, both_ref, rest_ref):
    tokens = direct_ref.shape[1] * 2 // 3
    chunk = out_ref.shape[2]

    def finish_head(h, span, sums, total):
        share = sums / total
        if h == 0:
            both_ref[span, :] = share
            return
        lane = lax.broadcasted_iota(jnp.int32, share.shape, 1)
        if h == 1:
            both_ref[span, :] = jnp.where(lane < HALF, both_ref[span, :], share)
            return
        whole = both_ref[span, :] + jnp.where(lane < HALF, share, 0.0)
        whole = whole.T
        whole = whole[:HALF] + whole[HALF:]
        for i in range(ROWS // chunk):
            out_ref[span.start // chunk + i] = whole[:, i * chunk : (i + 1) * chunk]

    @pl.when(flag_ref[1] > 0)
    def _():
        rest_ref[...] = carried_ref[...]

    @pl.when(flag_ref[1] == 0)
    def _():
        rest_ref[...] = plain_ref[...]

    def emit(h, span, peak, mixed):
        old_peak = peaks_ref[h, span, :]
        new_peak = jnp.maximum(old_peak, peak)
        kept, added = jnp.exp2(old_peak - new_peak), jnp.exp2(peak - new_peak)
        sums = sums_ref[h, span, :] * kept + mixed[:, :HS] * added
        total = totals_ref[h, span, :] * kept + mixed[:, HS:] * added
        finish_head(h, span, sums, total)

    @pl.when(flag_ref[0] > 0)
    def _():
        attend(split_ref, [(direct_ref, tokens, 0), (rest_ref, tokens, 0)], emit)

    @pl.when(flag_ref[0] == 0)
    def _():
        for h in range(3):
            for b in range(split_ref.shape[1] // ROWS):
                span = slice(b * ROWS, (b + 1) * ROWS)
                finish_head(h, span, sums_ref[h, span, :], totals_ref[h, span, :])


def cost(frames, count):
    return pl.CostEstimate(
        flops=frames * 12 * count * count * 256,
        bytes_accessed=4 * MIB,
        transcendentals=frames * 3 * count * count,
    )


def attend_near(own, mate):
    count = own.shape[0] * own.shape[1] * 2 // 5
    return pl.pallas_call(
        near_kernel,
        in_specs=[VMEM] * 2,
        out_specs=[VMEM] * 4,
        out_shape=[jax.ShapeDtypeStruct((3, count, HS), jnp.float32)] * 3
        + [jax.ShapeDtypeStruct((3, count, 2 * HS), jnp.bfloat16)],
        compiler_params=params(20),
        cost_estimate=cost(2, count),
        name="attend_near",
    )(own, mate)


def attend_far(flags, split, direct, plain, carried, state, groups):
    count = split.shape[1]
    return pl.pallas_call(
        far_kernel,
        in_specs=[SMEM] + [VMEM] * 7,
        out_specs=VMEM,
        out_shape=jax.ShapeDtypeStruct((groups, HALF, count // groups), jnp.float32),
        scratch_shapes=[pltpu.VMEM((count, HS), jnp.float32), pltpu.VMEM(plain.shape, jnp.bfloat16)],
        compiler_params=params(16),
        cost_estimate=cost(1, count),
        name="attend_far",
    )(flags, split, direct, plain, carried, *state)


def finish_kernel(position_ref, levels_ref, timesteps_ref, parts_ref, latent_ref, fresh_ref, velocity_ref, sent_ref):
    velocity = parts_ref[0]
    for s in range(1, parts_ref.shape[0]):
        velocity = velocity + parts_ref[s]
    level = levels_ref[0]
    step = timesteps_ref[jnp.maximum(level - 2, 0)] - timesteps_ref[level]
    velocity_ref[...] = velocity
    advanced = latent_ref[...] + (step.astype(jnp.float32) / 64.0) * velocity
    sent_ref[...] = jnp.where(position_ref[0] == 0, fresh_ref[...], advanced)


def finish(position, levels, timesteps, parts, latent_t, fresh_t):
    shape = jax.ShapeDtypeStruct(latent_t.shape, jnp.float32)
    return pl.pallas_call(
        finish_kernel,
        in_specs=[SMEM] * 3 + [VMEM] * 3,
        out_specs=[VMEM] * 2,
        out_shape=[shape, shape],
        compiler_params=params(2),
        name="finish",
    )(position, levels, timesteps, parts, latent_t, fresh_t)


def turned(pairs):
    return [(j, i) for i, j in pairs]


def on_device(queries, key_proj, values, latents, head_weight, levels, timesteps, fresh_noise):
    position = lax.axis_index("queue")
    length = lax.axis_size("queue")
    groups = lax.axis_size("seq")
    sent = pack(queries[0], key_proj[0], values[0], head_weight.T, groups)
    own = lax.all_to_all(sent, "seq", split_axis=0, concat_axis=0, tiled=True)
    kv = own[:, queries.shape[1] :]
    cut = groups * CUT // 8
    column = length // 4
    inner = [(i, i + 1) for i in range(1, length - 1, 2) if (i + 1) % column]
    cross = [(i, i + 1) for i in range(column - 1, length - 1, column)]
    along_z = [(i, i + column) for i, _ in cross] + [(j, j - column) for _, j in cross]
    along_y = [(i + column, j) for i, j in cross] + [(j - column, i) for i, j in cross]
    pairs = inner + cross
    direct = lax.ppermute(kv[:cut], "queue", pairs + turned(pairs))
    plain = lax.ppermute(kv[cut:], "queue", inner + turned(inner) + along_z)
    mates = [(i, i + 1) for i in range(0, length, 2)]
    mate = lax.ppermute(own, "queue", mates + turned(mates))
    carried = lax.ppermute(plain, "queue", along_y)
    place = position % column
    has_far = (position > 0) & (position < length - 1)
    at_cross = (place == 0) | (place == column - 1)
    flags = jnp.stack([has_far, at_cross]).astype(jnp.int32)
    *state, split = attend_near(own, mate)
    parts = attend_far(flags, split, direct, plain, carried, state, groups)
    parts = lax.all_to_all(parts, "seq", split_axis=0, concat_axis=0, tiled=True)
    velocity, sent = finish(
        position[None].astype(jnp.int32), levels, timesteps, parts, latents[0].T, fresh_noise.T
    )
    shifted = lax.ppermute(sent, "queue", [(i, (i - 1) % length) for i in range(length)])
    return (shifted.T[None], velocity.T[None])


def solution(mesh):
    in_specs = (
        P("queue", "seq", None),
        P("queue", "seq", None),
        P("queue", "seq", None),
        P("queue", "seq", None),
        P(),
        P("queue"),
        P(),
        P("seq", None),
    )
    out_specs = (P("queue", "seq", None), P("queue", "seq", None))
    return jax.shard_map(
        on_device, mesh=mesh, in_specs=in_specs, out_specs=out_specs, check_vma=False
    )
```

```python
import functools
import math

import jax
import jax.numpy as jnp
from jax import lax
from jax.experimental import pallas as pl
from jax.experimental.pallas import tpu as pltpu
from jax.sharding import PartitionSpec as P

HS = 128
HALF = 64
MIB = 1 << 20
ROWS = 256
PACK_MIB = 56
CUT = 6
NT = (((1,), (1,)), ((), ()))
VMEM = pl.BlockSpec(memory_space=pltpu.VMEM)
ANY = pl.BlockSpec(memory_space=pl.ANY)
HBM = pl.BlockSpec(memory_space=pltpu.HBM)
SMEM = pl.BlockSpec(memory_space=pltpu.SMEM)


def pack_kernel(position_ref, query_ref, key_ref, value_ref, weight_ref, out_ref, stage, value_buf, weight_buf, query_sem, key_sem, value_sem, weight_sem, out_sem):
    groups, rows, part = stage.shape
    tokens = rows * 2 // 5
    half = tokens // 2
    queries, keys, values, weights = [], [], [], []
    for s in range(groups):
        span = pl.ds(s * part, part)
        values.append(pltpu.make_async_copy(value_ref.at[:, span], value_buf.at[s], value_sem.at[s]))
        weights.append(pltpu.make_async_copy(weight_ref.at[:, span], weight_buf.at[s], weight_sem.at[s]))
        keys.append(pltpu.make_async_copy(key_ref.at[:, span], stage.at[s, pl.ds(tokens, tokens)], key_sem.at[s]))
        queries.append(pltpu.make_async_copy(query_ref.at[:, span], stage.at[s, pl.ds(0, tokens)], query_sem.at[s]))
        values[s].start()
        weights[s].start()
        keys[s].start()
        queries[s].start()
    zero = jnp.zeros((HALF, HS), jnp.bfloat16)

    def diagonal(x, y):
        return jnp.concatenate(
            [jnp.concatenate([x, zero], axis=1), jnp.concatenate([zero, y], axis=1)], axis=0
        )

    outs = []
    for s in range(groups):
        values[s].wait()
        weights[s].wait()
        weight = [weight_buf[s, :, h * HS : (h + 1) * HS] for h in range(3)]
        pair = lax.dot_general(
            value_buf[s, :, : 2 * HS],
            diagonal(weight[0], weight[1]),
            NT,
            preferred_element_type=jnp.float32,
        ).astype(jnp.bfloat16)
        last = jnp.concatenate([value_buf[s, :half, 2 * HS :], value_buf[s, half:, 2 * HS :]], axis=1)
        last = lax.dot_general(
            last, diagonal(weight[2], weight[2]), NT, preferred_element_type=jnp.float32
        ).astype(jnp.bfloat16)
        stage[s, 2 * tokens :, :HS] = pair[:half]
        stage[s, 2 * tokens :, HS : 2 * HS] = pair[half:]
        stage[s, 2 * tokens :, 2 * HS :] = last
        keys[s].wait()
        queries[s].wait()
        outs.append(pltpu.make_async_copy(stage.at[s], out_ref.at[s], out_sem.at[s]))
        outs[s].start()
    for out in outs:
        out.wait()


def params(mib):
    return pltpu.CompilerParams(vmem_limit_bytes=mib * MIB)


def pack(position, queries, keys, values, weight_t, groups):
    tokens, width = keys.shape
    part = width // groups
    return pl.pallas_call(
        pack_kernel,
        in_specs=[SMEM] + [HBM] * 4,
        out_specs=HBM,
        out_shape=jax.ShapeDtypeStruct((groups, tokens * 5 // 2, part), jnp.bfloat16),
        scratch_shapes=[
            pltpu.VMEM((groups, tokens * 5 // 2, part), jnp.bfloat16),
            pltpu.VMEM((groups, tokens, part), jnp.bfloat16),
            pltpu.VMEM((groups, HALF, part), jnp.bfloat16),
        ]
        + [pltpu.SemaphoreType.DMA((groups,))] * 5,
        compiler_params=params(PACK_MIB),
        name="pack",
    )(position, queries, keys, values, weight_t)


def scaled_queries(query_ref, split_ref):
    groups, rows, _ = query_ref.shape
    tokens = rows * 2 // 5
    scale = HS ** (-0.5) * math.log2(math.e)
    for h in range(3):
        q = query_ref[:, :tokens, h * HS : (h + 1) * HS].reshape(groups * tokens, HS)
        q = q.astype(jnp.float32) * scale
        high = q.astype(jnp.bfloat16)
        low = (q - high.astype(jnp.float32)).astype(jnp.bfloat16)
        split_ref[h, :, :HS] = high
        split_ref[h, :, HS:] = low


def keys_and_values(ref, tokens, start, h):
    groups = ref.shape[0]
    count = groups * tokens
    k = ref[:, start : start + tokens, h * HS : (h + 1) * HS].reshape(count, HS)
    start += tokens
    if h == 2:
        first = ref[:, start : start + tokens // 2, 2 * HS :]
        second = jnp.concatenate([first[:, :, HALF:], first[:, :, :HALF]], axis=2)
    else:
        first = ref[:, start : start + tokens // 2, :HS]
        second = ref[:, start : start + tokens // 2, HS : 2 * HS]
    mix = jnp.concatenate([first, second], axis=1).reshape(count, HS)
    return k, mix


def attend(split_ref, sources, emit):
    for h in range(3):
        parts = [keys_and_values(ref, tokens, start, h) for ref, tokens, start in sources]
        k = jnp.concatenate([part[0] for part in parts], axis=0)
        mix = jnp.concatenate([part[1] for part in parts], axis=0)
        k = jnp.concatenate([k, k], axis=1)
        mix = jnp.concatenate([mix, jnp.ones_like(mix)], axis=1)
        for b in range(split_ref.shape[1] // ROWS):
            span = slice(b * ROWS, (b + 1) * ROWS)
            scores = lax.dot_general(split_ref[h, span, :], k, NT, preferred_element_type=jnp.float32)
            peak = jnp.ceil(jnp.max(scores, axis=1, keepdims=True))
            probs = jnp.exp2(scores - peak).astype(jnp.bfloat16)
            emit(h, span, peak, jnp.dot(probs, mix, preferred_element_type=jnp.float32))


def cut_kernel(own_ref, direct_ref, rest_ref):
    cut, rows, _ = direct_ref.shape
    direct_ref[...] = own_ref[:cut, -rows:, :]
    rest_ref[...] = own_ref[cut:, -rows:, :]


def near_kernel(own_ref, mate_ref, split_ref, sums_ref, totals_ref, peaks_ref):
    scaled_queries(own_ref, split_ref)
    tokens = own_ref.shape[1] * 2 // 5

    def emit(h, span, peak, mixed):
        sums_ref[h, span, :] = mixed[:, :HS]
        totals_ref[h, span, :] = mixed[:, HS:]
        peaks_ref[h, span, :] = jnp.broadcast_to(peak, (ROWS, HS))

    attend(split_ref, [(own_ref, tokens, tokens), (mate_ref, tokens, tokens)], emit)


def pass_kernel(rest_ref, after_ref, out_ref):
    pass


def far_kernel(column, length, position_ref, split_ref, direct_ref, plain_ref, carried_ref, sums_ref, totals_ref, peaks_ref, out_ref, both_ref, rest_ref):
    position = position_ref[0]
    place = lax.rem(position, column)
    has_far = jnp.logical_and(position > 0, position < length - 1)
    at_cross = jnp.logical_or(place == 0, place == column - 1)
    tokens = direct_ref.shape[1] * 2 // 3
    chunk = out_ref.shape[2]

    def finish_head(h, span, sums, total):
        share = sums / total
        if h == 0:
            both_ref[span, :] = share
            return
        lane = lax.broadcasted_iota(jnp.int32, share.shape, 1)
        if h == 1:
            both_ref[span, :] = jnp.where(lane < HALF, both_ref[span, :], share)
            return
        whole = both_ref[span, :] + jnp.where(lane < HALF, share, 0.0)
        whole = whole.T
        whole = whole[:HALF] + whole[HALF:]
        for i in range(ROWS // chunk):
            out_ref[span.start // chunk + i] = whole[:, i * chunk : (i + 1) * chunk]

    @pl.when(at_cross)
    def _():
        rest_ref[...] = carried_ref[...]

    @pl.when(jnp.logical_not(at_cross))
    def _():
        rest_ref[...] = plain_ref[...]

    def emit(h, span, peak, mixed):
        peak = jnp.where(has_far, peak, -1e30)
        old_peak = peaks_ref[h, span, :]
        new_peak = jnp.maximum(old_peak, peak)
        kept, added = jnp.exp2(old_peak - new_peak), jnp.exp2(peak - new_peak)
        sums = sums_ref[h, span, :] * kept + mixed[:, :HS] * added
        total = totals_ref[h, span, :] * kept + mixed[:, HS:] * added
        finish_head(h, span, sums, total)

    attend(split_ref, [(direct_ref, tokens, 0), (rest_ref, tokens, 0)], emit)


def cost(frames, count):
    return pl.CostEstimate(
        flops=frames * 12 * count * count * 256,
        bytes_accessed=4 * MIB,
        transcendentals=frames * 3 * count * count,
    )


def cut_rows(own, cut):
    groups, rows, part = own.shape
    rows = rows * 3 // 5
    return pl.pallas_call(
        cut_kernel,
        in_specs=[VMEM],
        out_specs=[VMEM] * 2,
        out_shape=[jax.ShapeDtypeStruct((count, rows, part), own.dtype) for count in (cut, groups - cut)],
        compiler_params=params(2),
        name="cut_rows",
    )(own)


def passed_after(rest, after):
    return pl.pallas_call(
        pass_kernel,
        in_specs=[ANY] * 2,
        out_specs=ANY,
        out_shape=jax.ShapeDtypeStruct(rest.shape, rest.dtype),
        input_output_aliases={0: 0},
        compiler_params=params(2),
        name="passed_after",
    )(rest, after)


def attend_near(own, mate):
    count = own.shape[0] * own.shape[1] * 2 // 5
    return pl.pallas_call(
        near_kernel,
        in_specs=[VMEM] * 2,
        out_specs=[VMEM] * 4,
        out_shape=[jax.ShapeDtypeStruct((3, count, 2 * HS), jnp.bfloat16)]
        + [jax.ShapeDtypeStruct((3, count, HS), jnp.float32)] * 3,
        compiler_params=params(16),
        cost_estimate=cost(2, count),
        name="attend_near",
    )(own, mate)


def attend_far(position, split, direct, plain, carried, state, groups, column, length):
    count = split.shape[1]
    return pl.pallas_call(
        functools.partial(far_kernel, column, length),
        in_specs=[SMEM] + [VMEM] * 7,
        out_specs=VMEM,
        out_shape=jax.ShapeDtypeStruct((groups, HALF, count // groups), jnp.float32),
        scratch_shapes=[pltpu.VMEM((count, HS), jnp.float32), pltpu.VMEM(plain.shape, jnp.bfloat16)],
        compiler_params=params(16),
        cost_estimate=cost(1, count),
        name="attend_far",
    )(position, split, direct, plain, carried, *state)


def finish_kernel(position_ref, levels_ref, timesteps_ref, parts_ref, latent_ref, fresh_ref, velocity_ref, sent_ref):
    velocity = parts_ref[0]
    for s in range(1, parts_ref.shape[0]):
        velocity = velocity + parts_ref[s]
    level = levels_ref[0]
    step = timesteps_ref[jnp.maximum(level - 2, 0)] - timesteps_ref[level]
    velocity_ref[...] = velocity
    advanced = latent_ref[...] + (step.astype(jnp.float32) / 64.0) * velocity
    sent_ref[...] = jnp.where(position_ref[0] == 0, fresh_ref[...], advanced)


def finish(position, levels, timesteps, parts, latent_t, fresh_t):
    shape = jax.ShapeDtypeStruct(latent_t.shape, jnp.float32)
    return pl.pallas_call(
        finish_kernel,
        in_specs=[SMEM] * 3 + [VMEM] * 3,
        out_specs=[VMEM] * 2,
        out_shape=[shape, shape],
        compiler_params=params(2),
        name="finish",
    )(position, levels, timesteps, parts, latent_t, fresh_t)


def turned(pairs):
    return [(j, i) for i, j in pairs]


def on_device(queries, key_proj, values, latents, head_weight, levels, timesteps, fresh_noise):
    position = lax.axis_index("queue")[None].astype(jnp.int32)
    length = lax.axis_size("queue")
    groups = lax.axis_size("seq")
    sent = pack(position, queries[0], key_proj[0], values[0], head_weight.T, groups)
    own = lax.all_to_all(sent, "seq", split_axis=0, concat_axis=0, tiled=True)
    direct, rest = cut_rows(own, groups * CUT // 8)
    column = length // 4
    inner = [(i, i + 1) for i in range(1, length - 1, 2) if (i + 1) % column]
    cross = [(i, i + 1) for i in range(column - 1, length - 1, column)]
    along_z = [(i, i + column) for i, _ in cross] + [(j, j - column) for _, j in cross]
    along_y = [(i + column, j) for i, j in cross] + [(j - column, i) for i, j in cross]
    pairs = inner + cross
    direct = lax.ppermute(direct, "queue", pairs + turned(pairs))
    plain = lax.ppermute(rest, "queue", inner + turned(inner) + along_z)
    mates = [(i, i + 1) for i in range(0, length, 2)]
    mate = lax.ppermute(own, "queue", mates + turned(mates))
    split, *state = attend_near(own, mate)
    plain = passed_after(plain, split)
    carried = lax.ppermute(plain, "queue", along_y)
    parts = attend_far(position, split, direct, plain, carried, state, groups, column, length)
    parts = lax.all_to_all(parts, "seq", split_axis=0, concat_axis=0, tiled=True)
    velocity, sent = finish(
        position, levels, timesteps, parts, latents[0].T, fresh_noise.T
    )
    shifted = lax.ppermute(sent, "queue", [(i, (i - 1) % length) for i in range(length)])
    return (shifted.T[None], velocity.T[None])


def solution(mesh):
    in_specs = (
        P("queue", "seq", None),
        P("queue", "seq", None),
        P("queue", "seq", None),
        P("queue", "seq", None),
        P(),
        P("queue"),
        P(),
        P("seq", None),
    )
    out_specs = (P("queue", "seq", None), P("queue", "seq", None))
    return jax.shard_map(
        on_device, mesh=mesh, in_specs=in_specs, out_specs=out_specs, check_vma=False
    )
```

```python
import functools
import math

import jax
import jax.numpy as jnp
from jax import lax
from jax.experimental import pallas as pl
from jax.experimental.pallas import tpu as pltpu
from jax.sharding import PartitionSpec as P

HS = 128
HALF = 64
MIB = 1 << 20
ROWS = 256
PACK_MIB = 56
CUT = 5
NT = (((1,), (1,)), ((), ()))
VMEM = pl.BlockSpec(memory_space=pltpu.VMEM)
ANY = pl.BlockSpec(memory_space=pl.ANY)
HBM = pl.BlockSpec(memory_space=pltpu.HBM)
SMEM = pl.BlockSpec(memory_space=pltpu.SMEM)


def pack_kv_kernel(position_ref, key_ref, value_ref, weight_ref, out_ref, stage, value_buf, weight_buf, key_sem, value_sem, weight_sem, out_sem):
    groups, rows, part = stage.shape
    tokens = rows * 2 // 3
    half = tokens // 2
    keys, values, weights = [], [], []
    for s in range(groups):
        span = pl.ds(s * part, part)
        values.append(pltpu.make_async_copy(value_ref.at[:, span], value_buf.at[s], value_sem.at[s]))
        weights.append(pltpu.make_async_copy(weight_ref.at[:, span], weight_buf.at[s], weight_sem.at[s]))
        keys.append(pltpu.make_async_copy(key_ref.at[:, span], stage.at[s, pl.ds(0, tokens)], key_sem.at[s]))
        values[s].start()
        weights[s].start()
        keys[s].start()
    zero = jnp.zeros((HALF, HS), jnp.bfloat16)

    def diagonal(x, y):
        return jnp.concatenate(
            [jnp.concatenate([x, zero], axis=1), jnp.concatenate([zero, y], axis=1)], axis=0
        )

    outs = []
    for s in range(groups):
        values[s].wait()
        weights[s].wait()
        weight = [weight_buf[s, :, h * HS : (h + 1) * HS] for h in range(3)]
        pair = lax.dot_general(
            value_buf[s, :, : 2 * HS],
            diagonal(weight[0], weight[1]),
            NT,
            preferred_element_type=jnp.float32,
        ).astype(jnp.bfloat16)
        last = jnp.concatenate([value_buf[s, :half, 2 * HS :], value_buf[s, half:, 2 * HS :]], axis=1)
        last = lax.dot_general(
            last, diagonal(weight[2], weight[2]), NT, preferred_element_type=jnp.float32
        ).astype(jnp.bfloat16)
        stage[s, tokens:, :HS] = pair[:half]
        stage[s, tokens:, HS : 2 * HS] = pair[half:]
        stage[s, tokens:, 2 * HS :] = last
        keys[s].wait()
        outs.append(pltpu.make_async_copy(stage.at[s], out_ref.at[s], out_sem.at[s]))
        outs[s].start()
    for out in outs:
        out.wait()


def params(mib):
    return pltpu.CompilerParams(vmem_limit_bytes=mib * MIB)


def pack_kv(position, keys, values, weight_t, groups):
    tokens, width = keys.shape
    part = width // groups
    out = jax.ShapeDtypeStruct((groups, tokens * 3 // 2, part), jnp.bfloat16)
    return pl.pallas_call(
        pack_kv_kernel,
        in_specs=[SMEM] + [HBM] * 3,
        out_specs=HBM,
        out_shape=out,
        scratch_shapes=[
            pltpu.VMEM(out.shape, jnp.bfloat16),
            pltpu.VMEM((groups, tokens, part), jnp.bfloat16),
            pltpu.VMEM((groups, HALF, part), jnp.bfloat16),
        ]
        + [pltpu.SemaphoreType.DMA((groups,))] * 4,
        compiler_params=params(PACK_MIB),
        name="pack_kv",
    )(position, keys, values, weight_t)


def pack_q_kernel(query_ref, out_ref, sem):
    groups, _, part = out_ref.shape
    copies = [
        pltpu.make_async_copy(query_ref.at[:, pl.ds(s * part, part)], out_ref.at[s], sem.at[s])
        for s in range(groups)
    ]
    for copy in copies:
        copy.start()
    for copy in copies:
        copy.wait()


def pack_q(queries, groups):
    tokens, width = queries.shape
    part = width // groups
    return pl.pallas_call(
        pack_q_kernel,
        in_specs=[HBM],
        out_specs=VMEM,
        out_shape=jax.ShapeDtypeStruct((groups, tokens, part), jnp.bfloat16),
        scratch_shapes=[pltpu.SemaphoreType.DMA((groups,))],
        compiler_params=params(PACK_MIB),
        name="pack_q",
    )(queries)


def scaled_queries(query_ref, split_ref):
    groups, tokens, _ = query_ref.shape
    scale = HS ** (-0.5) * math.log2(math.e)
    for h in range(3):
        q = query_ref[:, :, h * HS : (h + 1) * HS].reshape(groups * tokens, HS)
        q = q.astype(jnp.float32) * scale
        high = q.astype(jnp.bfloat16)
        low = (q - high.astype(jnp.float32)).astype(jnp.bfloat16)
        split_ref[h, :, :HS] = high
        split_ref[h, :, HS:] = low


def keys_and_values(ref, tokens, start, h):
    groups = ref.shape[0]
    count = groups * tokens
    k = ref[:, start : start + tokens, h * HS : (h + 1) * HS].reshape(count, HS)
    start += tokens
    if h == 2:
        first = ref[:, start : start + tokens // 2, 2 * HS :]
        second = jnp.concatenate([first[:, :, HALF:], first[:, :, :HALF]], axis=2)
    else:
        first = ref[:, start : start + tokens // 2, :HS]
        second = ref[:, start : start + tokens // 2, HS : 2 * HS]
    mix = jnp.concatenate([first, second], axis=1).reshape(count, HS)
    return k, mix


def attend(split_ref, sources, emit):
    for h in range(3):
        parts = [keys_and_values(ref, tokens, start, h) for ref, tokens, start in sources]
        k = jnp.concatenate([part[0] for part in parts], axis=0)
        mix = jnp.concatenate([part[1] for part in parts], axis=0)
        k = jnp.concatenate([k, k], axis=1)
        mix = jnp.concatenate([mix, jnp.ones_like(mix)], axis=1)
        for b in range(split_ref.shape[1] // ROWS):
            span = slice(b * ROWS, (b + 1) * ROWS)
            scores = lax.dot_general(split_ref[h, span, :], k, NT, preferred_element_type=jnp.float32)
            peak = jnp.ceil(jnp.max(scores, axis=1, keepdims=True))
            probs = jnp.exp2(scores - peak).astype(jnp.bfloat16)
            emit(h, span, peak, jnp.dot(probs, mix, preferred_element_type=jnp.float32))


def cut_kernel(own_ref, direct_ref, rest_ref):
    cut = direct_ref.shape[0]
    direct_ref[...] = own_ref[:cut]
    rest_ref[...] = own_ref[cut:]


def near_kernel(query_ref, own_ref, mate_ref, split_ref, sums_ref, totals_ref, peaks_ref):
    scaled_queries(query_ref, split_ref)
    tokens = query_ref.shape[1]

    def emit(h, span, peak, mixed):
        sums_ref[h, span, :] = mixed[:, :HS]
        totals_ref[h, span, :] = mixed[:, HS:]
        peaks_ref[h, span, :] = jnp.broadcast_to(peak, (ROWS, HS))

    attend(split_ref, [(own_ref, tokens, 0), (mate_ref, tokens, 0)], emit)


def pass_kernel(rest_ref, after_ref, out_ref):
    pass


def far_kernel(column, length, position_ref, split_ref, direct_ref, plain_ref, carried_ref, sums_ref, totals_ref, peaks_ref, out_ref, both_ref, rest_ref):
    position = position_ref[0]
    place = lax.rem(position, column)
    has_far = jnp.logical_and(position > 0, position < length - 1)
    at_cross = jnp.logical_or(place == 0, place == column - 1)
    tokens = direct_ref.shape[1] * 2 // 3
    chunk = out_ref.shape[2]

    def finish_head(h, span, sums, total):
        share = sums / total
        if h == 0:
            both_ref[span, :] = share
            return
        lane = lax.broadcasted_iota(jnp.int32, share.shape, 1)
        if h == 1:
            both_ref[span, :] = jnp.where(lane < HALF, both_ref[span, :], share)
            return
        whole = both_ref[span, :] + jnp.where(lane < HALF, share, 0.0)
        whole = whole.T
        whole = whole[:HALF] + whole[HALF:]
        for i in range(ROWS // chunk):
            out_ref[span.start // chunk + i] = whole[:, i * chunk : (i + 1) * chunk]

    @pl.when(at_cross)
    def _():
        rest_ref[...] = carried_ref[...]

    @pl.when(jnp.logical_not(at_cross))
    def _():
        rest_ref[...] = plain_ref[...]

    def emit(h, span, peak, mixed):
        peak = jnp.where(has_far, peak, -1e30)
        old_peak = peaks_ref[h, span, :]
        new_peak = jnp.maximum(old_peak, peak)
        kept, added = jnp.exp2(old_peak - new_peak), jnp.exp2(peak - new_peak)
        sums = sums_ref[h, span, :] * kept + mixed[:, :HS] * added
        total = totals_ref[h, span, :] * kept + mixed[:, HS:] * added
        finish_head(h, span, sums, total)

    attend(split_ref, [(direct_ref, tokens, 0), (rest_ref, tokens, 0)], emit)


def cost(frames, count):
    return pl.CostEstimate(
        flops=frames * 12 * count * count * 256,
        bytes_accessed=4 * MIB,
        transcendentals=frames * 3 * count * count,
    )


def cut_rows(own, cut):
    groups, rows, part = own.shape
    return pl.pallas_call(
        cut_kernel,
        in_specs=[VMEM],
        out_specs=[VMEM] * 2,
        out_shape=[jax.ShapeDtypeStruct((count, rows, part), own.dtype) for count in (cut, groups - cut)],
        compiler_params=params(2),
        name="cut_rows",
    )(own)


def passed_after(rest, after):
    return pl.pallas_call(
        pass_kernel,
        in_specs=[ANY] * 2,
        out_specs=ANY,
        out_shape=jax.ShapeDtypeStruct(rest.shape, rest.dtype),
        input_output_aliases={0: 0},
        compiler_params=params(2),
        name="passed_after",
    )(rest, after)


def attend_near(q, own, mate):
    count = q.shape[0] * q.shape[1]
    return pl.pallas_call(
        near_kernel,
        in_specs=[VMEM] * 3,
        out_specs=[VMEM] * 4,
        out_shape=[jax.ShapeDtypeStruct((3, count, 2 * HS), jnp.bfloat16)]
        + [jax.ShapeDtypeStruct((3, count, HS), jnp.float32)] * 3,
        compiler_params=params(16),
        cost_estimate=cost(2, count),
        name="attend_near",
    )(q, own, mate)


def attend_far(position, split, direct, plain, carried, state, groups, column, length):
    count = split.shape[1]
    return pl.pallas_call(
        functools.partial(far_kernel, column, length),
        in_specs=[SMEM] + [VMEM] * 7,
        out_specs=VMEM,
        out_shape=jax.ShapeDtypeStruct((groups, HALF, count // groups), jnp.float32),
        scratch_shapes=[pltpu.VMEM((count, HS), jnp.float32), pltpu.VMEM(plain.shape, jnp.bfloat16)],
        compiler_params=params(16),
        cost_estimate=cost(1, count),
        name="attend_far",
    )(position, split, direct, plain, carried, *state)


def finish_kernel(position_ref, levels_ref, timesteps_ref, parts_ref, latent_ref, fresh_ref, velocity_ref, sent_ref):
    velocity = parts_ref[0]
    for s in range(1, parts_ref.shape[0]):
        velocity = velocity + parts_ref[s]
    level = levels_ref[0]
    step = timesteps_ref[jnp.maximum(level - 2, 0)] - timesteps_ref[level]
    velocity_ref[...] = velocity
    advanced = latent_ref[...] + (step.astype(jnp.float32) / 64.0) * velocity
    sent_ref[...] = jnp.where(position_ref[0] == 0, fresh_ref[...], advanced)


def finish(position, levels, timesteps, parts, latent_t, fresh_t):
    shape = jax.ShapeDtypeStruct(latent_t.shape, jnp.float32)
    return pl.pallas_call(
        finish_kernel,
        in_specs=[SMEM] * 3 + [VMEM] * 3,
        out_specs=[VMEM] * 2,
        out_shape=[shape, shape],
        compiler_params=params(2),
        name="finish",
    )(position, levels, timesteps, parts, latent_t, fresh_t)


def turned(pairs):
    return [(j, i) for i, j in pairs]


def on_device(queries, key_proj, values, latents, head_weight, levels, timesteps, fresh_noise):
    position = lax.axis_index("queue")[None].astype(jnp.int32)
    length = lax.axis_size("queue")
    groups = lax.axis_size("seq")
    own = pack_kv(position, key_proj[0], values[0], head_weight.T, groups)
    own = lax.all_to_all(own, "seq", split_axis=0, concat_axis=0, tiled=True)
    first, rest = cut_rows(own, groups * CUT // 8)
    column = length // 4
    inner = [(i, i + 1) for i in range(1, length - 1, 2) if (i + 1) % column]
    cross = [(i, i + 1) for i in range(column - 1, length - 1, column)]
    along_z = [(i, i + column) for i, _ in cross] + [(j, j - column) for _, j in cross]
    along_y = [(i + column, j) for i, j in cross] + [(j - column, i) for i, j in cross]
    pairs = inner + cross
    direct = lax.ppermute(first, "queue", pairs + turned(pairs))
    plain = lax.ppermute(rest, "queue", inner + turned(inner) + along_z)
    mates = [(i, i + 1) for i in range(0, length, 2)]
    mate = lax.ppermute(own, "queue", mates + turned(mates))
    q = passed_after(pack_q(queries[0], groups), first)
    q = lax.all_to_all(q, "seq", split_axis=0, concat_axis=0, tiled=True)
    split, *state = attend_near(q, own, mate)
    plain = passed_after(plain, split)
    carried = lax.ppermute(plain, "queue", along_y)
    parts = attend_far(position, split, direct, plain, carried, state, groups, column, length)
    parts = lax.all_to_all(parts, "seq", split_axis=0, concat_axis=0, tiled=True)
    velocity, sent = finish(
        position, levels, timesteps, parts, latents[0].T, fresh_noise.T
    )
    shifted = lax.ppermute(sent, "queue", [(i, (i - 1) % length) for i in range(length)])
    return (shifted.T[None], velocity.T[None])


def solution(mesh):
    in_specs = (
        P("queue", "seq", None),
        P("queue", "seq", None),
        P("queue", "seq", None),
        P("queue", "seq", None),
        P(),
        P("queue"),
        P(),
        P("seq", None),
    )
    out_specs = (P("queue", "seq", None), P("queue", "seq", None))
    return jax.shard_map(
        on_device, mesh=mesh, in_specs=in_specs, out_specs=out_specs, check_vma=False
    )
```

```python
import functools
import math

import jax
import jax.numpy as jnp
from jax import lax
from jax.experimental import pallas as pl
from jax.experimental.pallas import tpu as pltpu
from jax.sharding import PartitionSpec as P

HS = 128
HALF = 64
MIB = 1 << 20
ROWS = 256
PACK_MIB = 56
CUT = 6
NT = (((1,), (1,)), ((), ()))
VMEM = pl.BlockSpec(memory_space=pltpu.VMEM)
ANY = pl.BlockSpec(memory_space=pl.ANY)
HBM = pl.BlockSpec(memory_space=pltpu.HBM)
SMEM = pl.BlockSpec(memory_space=pltpu.SMEM)


def pack_kernel(position_ref, query_ref, key_ref, value_ref, weight_ref, out_ref, stage, value_buf, weight_buf, query_sem, key_sem, value_sem, weight_sem, out_sem, mixed_sem):
    groups, rows, part = stage.shape
    tokens = rows * 2 // 5
    half = tokens // 2
    queries, keys, values, weights, outs, mixes = [], [], [], [], [], []
    for s in range(groups):
        span = pl.ds(s * part, part)
        moved, mixed = pl.ds(0, 2 * tokens), pl.ds(2 * tokens, half)
        values.append(pltpu.make_async_copy(value_ref.at[:, span], value_buf.at[s], value_sem.at[s]))
        weights.append(pltpu.make_async_copy(weight_ref.at[:, span], weight_buf.at[s], weight_sem.at[s]))
        keys.append(pltpu.make_async_copy(key_ref.at[:, span], stage.at[s, pl.ds(tokens, tokens)], key_sem.at[s]))
        queries.append(pltpu.make_async_copy(query_ref.at[:, span], stage.at[s, pl.ds(0, tokens)], query_sem.at[s]))
        outs.append(pltpu.make_async_copy(stage.at[s, moved], out_ref.at[s, moved], out_sem.at[s]))
        mixes.append(pltpu.make_async_copy(stage.at[s, mixed], out_ref.at[s, mixed], mixed_sem.at[s]))
    for s in range(groups):
        values[s].start()
        weights[s].start()
    for s in range(groups):
        keys[s].start()
        queries[s].start()
    for s in range(groups):
        values[s].wait()
        weights[s].wait()
    for s in range(groups):
        keys[s].wait()
        queries[s].wait()
        outs[s].start()
    zero = jnp.zeros((HALF, HS), jnp.bfloat16)

    def diagonal(x, y):
        return jnp.concatenate(
            [jnp.concatenate([x, zero], axis=1), jnp.concatenate([zero, y], axis=1)], axis=0
        )

    for s in range(groups):
        weight = [weight_buf[s, :, h * HS : (h + 1) * HS] for h in range(3)]
        pair = lax.dot_general(
            value_buf[s, :, : 2 * HS],
            diagonal(weight[0], weight[1]),
            NT,
            preferred_element_type=jnp.float32,
        ).astype(jnp.bfloat16)
        last = jnp.concatenate([value_buf[s, :half, 2 * HS :], value_buf[s, half:, 2 * HS :]], axis=1)
        last = lax.dot_general(
            last, diagonal(weight[2], weight[2]), NT, preferred_element_type=jnp.float32
        ).astype(jnp.bfloat16)
        stage[s, 2 * tokens :, :HS] = pair[:half]
        stage[s, 2 * tokens :, HS : 2 * HS] = pair[half:]
        stage[s, 2 * tokens :, 2 * HS :] = last
    for s in range(groups):
        mixes[s].start()
    for s in range(groups):
        outs[s].wait()
        mixes[s].wait()


def params(mib):
    return pltpu.CompilerParams(vmem_limit_bytes=mib * MIB)


def pack(position, queries, keys, values, weight_t, groups):
    tokens, width = keys.shape
    part = width // groups
    return pl.pallas_call(
        pack_kernel,
        in_specs=[SMEM] + [HBM] * 4,
        out_specs=HBM,
        out_shape=jax.ShapeDtypeStruct((groups, tokens * 5 // 2, part), jnp.bfloat16),
        scratch_shapes=[
            pltpu.VMEM((groups, tokens * 5 // 2, part), jnp.bfloat16),
            pltpu.VMEM((groups, tokens, part), jnp.bfloat16),
            pltpu.VMEM((groups, HALF, part), jnp.bfloat16),
        ]
        + [pltpu.SemaphoreType.DMA((groups,))] * 6,
        compiler_params=params(PACK_MIB),
        name="pack",
    )(position, queries, keys, values, weight_t)


def scaled_queries(query_ref, split_ref):
    groups, rows, _ = query_ref.shape
    tokens = rows * 2 // 5
    scale = HS ** (-0.5) * math.log2(math.e)
    for h in range(3):
        q = query_ref[:, :tokens, h * HS : (h + 1) * HS].reshape(groups * tokens, HS)
        q = q.astype(jnp.float32) * scale
        high = q.astype(jnp.bfloat16)
        low = (q - high.astype(jnp.float32)).astype(jnp.bfloat16)
        split_ref[h, :, :HS] = high
        split_ref[h, :, HS:] = low


def keys_and_values(ref, tokens, start, h):
    groups = ref.shape[0]
    count = groups * tokens
    k = ref[:, start : start + tokens, h * HS : (h + 1) * HS].reshape(count, HS)
    start += tokens
    if h == 2:
        first = ref[:, start : start + tokens // 2, 2 * HS :]
        second = jnp.concatenate([first[:, :, HALF:], first[:, :, :HALF]], axis=2)
    else:
        first = ref[:, start : start + tokens // 2, :HS]
        second = ref[:, start : start + tokens // 2, HS : 2 * HS]
    mix = jnp.concatenate([first, second], axis=1).reshape(count, HS)
    return k, mix


def attend(split_ref, sources, emit):
    for h in range(3):
        parts = [keys_and_values(ref, tokens, start, h) for ref, tokens, start in sources]
        k = jnp.concatenate([part[0] for part in parts], axis=0)
        mix = jnp.concatenate([part[1] for part in parts], axis=0)
        k = jnp.concatenate([k, k], axis=1)
        mix = jnp.concatenate([mix, jnp.ones_like(mix)], axis=1)
        for b in range(split_ref.shape[1] // ROWS):
            span = slice(b * ROWS, (b + 1) * ROWS)
            scores = lax.dot_general(split_ref[h, span, :], k, NT, preferred_element_type=jnp.float32)
            peak = jnp.ceil(jnp.max(scores, axis=1, keepdims=True))
            probs = jnp.exp2(scores - peak).astype(jnp.bfloat16)
            emit(h, span, peak, jnp.dot(probs, mix, preferred_element_type=jnp.float32))


def cut_kernel(own_ref, direct_ref, rest_ref):
    cut, rows, _ = direct_ref.shape
    direct_ref[...] = own_ref[:cut, -rows:, :]
    rest_ref[...] = own_ref[cut:, -rows:, :]


def near_kernel(own_ref, mate_ref, split_ref, sums_ref, totals_ref, peaks_ref):
    scaled_queries(own_ref, split_ref)
    tokens = own_ref.shape[1] * 2 // 5

    def emit(h, span, peak, mixed):
        sums_ref[h, span, :] = mixed[:, :HS]
        totals_ref[h, span, :] = mixed[:, HS:]
        peaks_ref[h, span, :] = jnp.broadcast_to(peak, (ROWS, HS))

    attend(split_ref, [(own_ref, tokens, tokens), (mate_ref, tokens, tokens)], emit)


def pass_kernel(rest_ref, after_ref, out_ref):
    pass


def far_kernel(column, length, position_ref, split_ref, direct_ref, plain_ref, carried_ref, sums_ref, totals_ref, peaks_ref, out_ref, both_ref, rest_ref):
    position = position_ref[0]
    place = lax.rem(position, column)
    has_far = jnp.logical_and(position > 0, position < length - 1)
    at_cross = jnp.logical_or(place == 0, place == column - 1)
    tokens = direct_ref.shape[1] * 2 // 3
    chunk = out_ref.shape[2]

    def finish_head(h, span, sums, total):
        share = sums / total
        if h == 0:
            both_ref[span, :] = share
            return
        lane = lax.broadcasted_iota(jnp.int32, share.shape, 1)
        if h == 1:
            both_ref[span, :] = jnp.where(lane < HALF, both_ref[span, :], share)
            return
        whole = both_ref[span, :] + jnp.where(lane < HALF, share, 0.0)
        whole = whole.T
        whole = whole[:HALF] + whole[HALF:]
        for i in range(ROWS // chunk):
            out_ref[span.start // chunk + i] = whole[:, i * chunk : (i + 1) * chunk]

    @pl.when(at_cross)
    def _():
        rest_ref[...] = carried_ref[...]

    @pl.when(jnp.logical_not(at_cross))
    def _():
        rest_ref[...] = plain_ref[...]

    def emit(h, span, peak, mixed):
        peak = jnp.where(has_far, peak, -1e30)
        old_peak = peaks_ref[h, span, :]
        new_peak = jnp.maximum(old_peak, peak)
        kept, added = jnp.exp2(old_peak - new_peak), jnp.exp2(peak - new_peak)
        sums = sums_ref[h, span, :] * kept + mixed[:, :HS] * added
        total = totals_ref[h, span, :] * kept + mixed[:, HS:] * added
        finish_head(h, span, sums, total)

    attend(split_ref, [(direct_ref, tokens, 0), (rest_ref, tokens, 0)], emit)


def cost(frames, count):
    return pl.CostEstimate(
        flops=frames * 12 * count * count * 256,
        bytes_accessed=4 * MIB,
        transcendentals=frames * 3 * count * count,
    )


def cut_rows(own, cut):
    groups, rows, part = own.shape
    rows = rows * 3 // 5
    return pl.pallas_call(
        cut_kernel,
        in_specs=[VMEM],
        out_specs=[VMEM] * 2,
        out_shape=[jax.ShapeDtypeStruct((count, rows, part), own.dtype) for count in (cut, groups - cut)],
        compiler_params=params(2),
        name="cut_rows",
    )(own)


def passed_after(rest, after):
    return pl.pallas_call(
        pass_kernel,
        in_specs=[ANY] * 2,
        out_specs=ANY,
        out_shape=jax.ShapeDtypeStruct(rest.shape, rest.dtype),
        input_output_aliases={0: 0},
        compiler_params=params(2),
        name="passed_after",
    )(rest, after)


def attend_near(own, mate):
    count = own.shape[0] * own.shape[1] * 2 // 5
    return pl.pallas_call(
        near_kernel,
        in_specs=[VMEM] * 2,
        out_specs=[VMEM] * 4,
        out_shape=[jax.ShapeDtypeStruct((3, count, 2 * HS), jnp.bfloat16)]
        + [jax.ShapeDtypeStruct((3, count, HS), jnp.float32)] * 3,
        compiler_params=params(16),
        cost_estimate=cost(0, count),
        name="attend_near",
    )(own, mate)


def attend_far(position, split, direct, plain, carried, state, groups, column, length):
    count = split.shape[1]
    return pl.pallas_call(
        functools.partial(far_kernel, column, length),
        in_specs=[SMEM] + [VMEM] * 7,
        out_specs=VMEM,
        out_shape=jax.ShapeDtypeStruct((groups, HALF, count // groups), jnp.float32),
        scratch_shapes=[pltpu.VMEM((count, HS), jnp.float32), pltpu.VMEM(plain.shape, jnp.bfloat16)],
        compiler_params=params(16),
        cost_estimate=cost(1, count),
        name="attend_far",
    )(position, split, direct, plain, carried, *state)


def summed(parts_ref):
    velocity = parts_ref[0]
    for s in range(1, parts_ref.shape[0]):
        velocity = velocity + parts_ref[s]
    return velocity


def velocity_kernel(parts_ref, velocity_ref):
    velocity_ref[...] = summed(parts_ref)


def advance_kernel(position_ref, levels_ref, timesteps_ref, parts_ref, latent_ref, fresh_ref, sent_ref):
    level = levels_ref[0]
    step = timesteps_ref[jnp.maximum(level - 2, 0)] - timesteps_ref[level]
    advanced = latent_ref[...] + (step.astype(jnp.float32) / 64.0) * summed(parts_ref)
    sent_ref[...] = jnp.where(position_ref[0] == 0, fresh_ref[...], advanced)


def advance(position, levels, timesteps, parts, latent_t, fresh_t):
    return pl.pallas_call(
        advance_kernel,
        in_specs=[SMEM] * 3 + [VMEM] * 3,
        out_specs=VMEM,
        out_shape=jax.ShapeDtypeStruct(latent_t.shape, jnp.float32),
        compiler_params=params(2),
        name="advance",
    )(position, levels, timesteps, parts, latent_t, fresh_t)


def total_velocity(parts):
    return pl.pallas_call(
        velocity_kernel,
        in_specs=[VMEM],
        out_specs=VMEM,
        out_shape=jax.ShapeDtypeStruct(parts.shape[1:], jnp.float32),
        compiler_params=params(2),
        name="velocity",
    )(parts)


def turned(pairs):
    return [(j, i) for i, j in pairs]


def on_device(queries, key_proj, values, latents, head_weight, levels, timesteps, fresh_noise):
    position = lax.axis_index("queue")[None].astype(jnp.int32)
    length = lax.axis_size("queue")
    groups = lax.axis_size("seq")
    sent = pack(position, queries[0], key_proj[0], values[0], head_weight.T, groups)
    own = lax.all_to_all(sent, "seq", split_axis=0, concat_axis=0, tiled=True)
    direct, rest = cut_rows(own, groups * CUT // 8)
    column = length // 4
    inner = [(i, i + 1) for i in range(1, length - 1, 2) if (i + 1) % column]
    cross = [(i, i + 1) for i in range(column - 1, length - 1, column)]
    along_z = [(i, i + column) for i, _ in cross] + [(j, j - column) for _, j in cross]
    along_y = [(i + column, j) for i, j in cross] + [(j - column, i) for i, j in cross]
    pairs = inner + cross
    direct = lax.ppermute(direct, "queue", pairs + turned(pairs))
    plain = lax.ppermute(rest, "queue", inner + turned(inner) + along_z)
    mates = [(i, i + 1) for i in range(0, length, 2)]
    mate = lax.ppermute(own, "queue", mates + turned(mates))
    split, *state = attend_near(own, mate)
    plain = passed_after(plain, split)
    carried = lax.ppermute(plain, "queue", along_y)
    parts = attend_far(position, split, direct, plain, carried, state, groups, column, length)
    parts = lax.all_to_all(parts, "seq", split_axis=0, concat_axis=0, tiled=True)
    sent = advance(position, levels, timesteps, parts, latents[0].T, fresh_noise.T)
    shifted = lax.ppermute(sent, "queue", [(i, (i - 1) % length) for i in range(length)])
    return (shifted.T[None], total_velocity(parts).T[None])


def solution(mesh):
    in_specs = (
        P("queue", "seq", None),
        P("queue", "seq", None),
        P("queue", "seq", None),
        P("queue", "seq", None),
        P(),
        P("queue"),
        P(),
        P("seq", None),
    )
    out_specs = (P("queue", "seq", None), P("queue", "seq", None))
    return jax.shard_map(
        on_device, mesh=mesh, in_specs=in_specs, out_specs=out_specs, check_vma=False
    )
```

```python
import functools
import math

import jax
import jax.numpy as jnp
from jax import lax
from jax.experimental import pallas as pl
from jax.experimental.pallas import tpu as pltpu
from jax.sharding import PartitionSpec as P

HS = 128
HALF = 64
MIB = 1 << 20
ROWS = 256
PACK_MIB = 56
CUT = 6
MATES = 2
NT = (((1,), (1,)), ((), ()))
VMEM = pl.BlockSpec(memory_space=pltpu.VMEM)
ANY = pl.BlockSpec(memory_space=pl.ANY)
HBM = pl.BlockSpec(memory_space=pltpu.HBM)
SMEM = pl.BlockSpec(memory_space=pltpu.SMEM)


def pack_kernel(position_ref, query_ref, key_ref, value_ref, weight_ref, out_ref, stage, value_buf, weight_buf, query_sem, key_sem, value_sem, weight_sem, out_sem, mixed_sem):
    groups, rows, part = stage.shape
    tokens = rows * 2 // 5
    half = tokens // 2
    queries, keys, values, weights, outs, mixes = [], [], [], [], [], []
    for s in range(groups):
        span = pl.ds(s * part, part)
        moved, mixed = pl.ds(0, 2 * tokens), pl.ds(2 * tokens, half)
        values.append(pltpu.make_async_copy(value_ref.at[:, span], value_buf.at[s], value_sem.at[s]))
        weights.append(pltpu.make_async_copy(weight_ref.at[:, span], weight_buf.at[s], weight_sem.at[s]))
        keys.append(pltpu.make_async_copy(key_ref.at[:, span], stage.at[s, pl.ds(tokens, tokens)], key_sem.at[s]))
        queries.append(pltpu.make_async_copy(query_ref.at[:, span], stage.at[s, pl.ds(0, tokens)], query_sem.at[s]))
        outs.append(pltpu.make_async_copy(stage.at[s, moved], out_ref.at[s, moved], out_sem.at[s]))
        mixes.append(pltpu.make_async_copy(stage.at[s, mixed], out_ref.at[s, mixed], mixed_sem.at[s]))
    for s in range(groups):
        values[s].start()
        weights[s].start()
    for s in range(groups):
        keys[s].start()
        queries[s].start()
    for s in range(groups):
        values[s].wait()
        weights[s].wait()
    for s in range(groups):
        keys[s].wait()
        queries[s].wait()
        outs[s].start()
    zero = jnp.zeros((HALF, HS), jnp.bfloat16)

    def diagonal(x, y):
        return jnp.concatenate(
            [jnp.concatenate([x, zero], axis=1), jnp.concatenate([zero, y], axis=1)], axis=0
        )

    for s in range(groups):
        weight = [weight_buf[s, :, h * HS : (h + 1) * HS] for h in range(3)]
        pair = lax.dot_general(
            value_buf[s, :, : 2 * HS],
            diagonal(weight[0], weight[1]),
            NT,
            preferred_element_type=jnp.float32,
        ).astype(jnp.bfloat16)
        last = jnp.concatenate([value_buf[s, :half, 2 * HS :], value_buf[s, half:, 2 * HS :]], axis=1)
        last = lax.dot_general(
            last, diagonal(weight[2], weight[2]), NT, preferred_element_type=jnp.float32
        ).astype(jnp.bfloat16)
        stage[s, 2 * tokens :, :HS] = pair[:half]
        stage[s, 2 * tokens :, HS : 2 * HS] = pair[half:]
        stage[s, 2 * tokens :, 2 * HS :] = last
    for s in range(groups):
        mixes[s].start()
    for s in range(groups):
        outs[s].wait()
        mixes[s].wait()


def params(mib):
    return pltpu.CompilerParams(vmem_limit_bytes=mib * MIB)


def pack(position, queries, keys, values, weight_t, groups):
    tokens, width = keys.shape
    part = width // groups
    return pl.pallas_call(
        pack_kernel,
        in_specs=[SMEM] + [HBM] * 4,
        out_specs=HBM,
        out_shape=jax.ShapeDtypeStruct((groups, tokens * 5 // 2, part), jnp.bfloat16),
        scratch_shapes=[
            pltpu.VMEM((groups, tokens * 5 // 2, part), jnp.bfloat16),
            pltpu.VMEM((groups, tokens, part), jnp.bfloat16),
            pltpu.VMEM((groups, HALF, part), jnp.bfloat16),
        ]
        + [pltpu.SemaphoreType.DMA((groups,))] * 6,
        compiler_params=params(PACK_MIB),
        name="pack",
    )(position, queries, keys, values, weight_t)


def scaled_queries(query_ref, split_ref):
    groups, rows, _ = query_ref.shape
    tokens = rows * 2 // 5
    scale = HS ** (-0.5) * math.log2(math.e)
    for h in range(3):
        q = query_ref[:, :tokens, h * HS : (h + 1) * HS].reshape(groups * tokens, HS)
        q = q.astype(jnp.float32) * scale
        high = q.astype(jnp.bfloat16)
        low = (q - high.astype(jnp.float32)).astype(jnp.bfloat16)
        split_ref[h, :, :HS] = high
        split_ref[h, :, HS:] = low


def keys_and_values(ref, tokens, start, h):
    groups = ref.shape[0]
    count = groups * tokens
    k = ref[:, start : start + tokens, h * HS : (h + 1) * HS].reshape(count, HS)
    start += tokens
    if h == 2:
        first = ref[:, start : start + tokens // 2, 2 * HS :]
        second = jnp.concatenate([first[:, :, HALF:], first[:, :, :HALF]], axis=2)
    else:
        first = ref[:, start : start + tokens // 2, :HS]
        second = ref[:, start : start + tokens // 2, HS : 2 * HS]
    mix = jnp.concatenate([first, second], axis=1).reshape(count, HS)
    return k, mix


def attend(split_ref, sources, emit):
    for h in range(3):
        parts = [keys_and_values(ref, tokens, start, h) for ref, tokens, start in sources]
        k = jnp.concatenate([part[0] for part in parts], axis=0)
        mix = jnp.concatenate([part[1] for part in parts], axis=0)
        k = jnp.concatenate([k, k], axis=1)
        mix = jnp.concatenate([mix, jnp.ones_like(mix)], axis=1)
        for b in range(split_ref.shape[1] // ROWS):
            span = slice(b * ROWS, (b + 1) * ROWS)
            scores = lax.dot_general(split_ref[h, span, :], k, NT, preferred_element_type=jnp.float32)
            peak = jnp.ceil(jnp.max(scores, axis=1, keepdims=True))
            probs = jnp.exp2(scores - peak).astype(jnp.bfloat16)
            emit(h, span, peak, jnp.dot(probs, mix, preferred_element_type=jnp.float32))


def cut_kernel(own_ref, direct_ref, rest_ref, *mate_refs):
    cut, rows, _ = direct_ref.shape
    direct_ref[...] = own_ref[:cut, -rows:, :]
    rest_ref[...] = own_ref[cut:, -rows:, :]
    size = mate_refs[0].shape[0]
    for i, ref in enumerate(mate_refs):
        ref[...] = own_ref[i * size : (i + 1) * size, -rows:, :]


def own_kernel(own_ref, split_ref, sums_ref, totals_ref, peaks_ref):
    scaled_queries(own_ref, split_ref)
    tokens = own_ref.shape[1] * 2 // 5

    def emit(h, span, peak, mixed):
        sums_ref[h, span, :] = mixed[:, :HS]
        totals_ref[h, span, :] = mixed[:, HS:]
        peaks_ref[h, span, :] = jnp.broadcast_to(peak, (ROWS, HS))

    attend(split_ref, [(own_ref, tokens, tokens)], emit)


def mate_kernel(split_ref, *refs):
    *mate_refs, old_sums_ref, old_totals_ref, old_peaks_ref, sums_ref, totals_ref, peaks_ref = refs
    tokens = mate_refs[0].shape[1] * 2 // 3

    def emit(h, span, peak, mixed):
        old_peak = old_peaks_ref[h, span, :]
        new_peak = jnp.maximum(old_peak, peak)
        kept, added = jnp.exp2(old_peak - new_peak), jnp.exp2(peak - new_peak)
        sums_ref[h, span, :] = old_sums_ref[h, span, :] * kept + mixed[:, :HS] * added
        totals_ref[h, span, :] = old_totals_ref[h, span, :] * kept + mixed[:, HS:] * added
        peaks_ref[h, span, :] = new_peak

    attend(split_ref, [(ref, tokens, 0) for ref in mate_refs], emit)


def pass_kernel(rest_ref, after_ref, out_ref):
    pass


def far_kernel(column, length, position_ref, split_ref, direct_ref, plain_ref, carried_ref, sums_ref, totals_ref, peaks_ref, out_ref, both_ref, rest_ref):
    position = position_ref[0]
    place = lax.rem(position, column)
    has_far = jnp.logical_and(position > 0, position < length - 1)
    at_cross = jnp.logical_or(place == 0, place == column - 1)
    tokens = direct_ref.shape[1] * 2 // 3
    chunk = out_ref.shape[2]

    def finish_head(h, span, sums, total):
        share = sums / total
        if h == 0:
            both_ref[span, :] = share
            return
        lane = lax.broadcasted_iota(jnp.int32, share.shape, 1)
        if h == 1:
            both_ref[span, :] = jnp.where(lane < HALF, both_ref[span, :], share)
            return
        whole = both_ref[span, :] + jnp.where(lane < HALF, share, 0.0)
        whole = whole.T
        whole = whole[:HALF] + whole[HALF:]
        for i in range(ROWS // chunk):
            out_ref[span.start // chunk + i] = whole[:, i * chunk : (i + 1) * chunk]

    @pl.when(at_cross)
    def _():
        rest_ref[...] = carried_ref[...]

    @pl.when(jnp.logical_not(at_cross))
    def _():
        rest_ref[...] = plain_ref[...]

    def emit(h, span, peak, mixed):
        peak = jnp.where(has_far, peak, -1e30)
        old_peak = peaks_ref[h, span, :]
        new_peak = jnp.maximum(old_peak, peak)
        kept, added = jnp.exp2(old_peak - new_peak), jnp.exp2(peak - new_peak)
        sums = sums_ref[h, span, :] * kept + mixed[:, :HS] * added
        total = totals_ref[h, span, :] * kept + mixed[:, HS:] * added
        finish_head(h, span, sums, total)

    attend(split_ref, [(direct_ref, tokens, 0), (rest_ref, tokens, 0)], emit)


def cost(frames, count):
    return pl.CostEstimate(
        flops=frames * 12 * count * count * 256,
        bytes_accessed=4 * MIB,
        transcendentals=frames * 3 * count * count,
    )


def cut_rows(own, cut):
    groups, rows, part = own.shape
    rows = rows * 3 // 5
    return pl.pallas_call(
        cut_kernel,
        in_specs=[VMEM],
        out_specs=[VMEM] * (2 + MATES),
        out_shape=[
            jax.ShapeDtypeStruct((count, rows, part), own.dtype)
            for count in [cut, groups - cut] + [groups // MATES] * MATES
        ],
        compiler_params=params(2),
        name="cut_rows",
    )(own)


def passed_after(rest, after):
    return pl.pallas_call(
        pass_kernel,
        in_specs=[ANY] * 2,
        out_specs=ANY,
        out_shape=jax.ShapeDtypeStruct(rest.shape, rest.dtype),
        input_output_aliases={0: 0},
        compiler_params=params(2),
        name="passed_after",
    )(rest, after)


def attend_own(own):
    count = own.shape[0] * own.shape[1] * 2 // 5
    return pl.pallas_call(
        own_kernel,
        in_specs=[VMEM],
        out_specs=[VMEM] * 4,
        out_shape=[jax.ShapeDtypeStruct((3, count, 2 * HS), jnp.bfloat16)]
        + [jax.ShapeDtypeStruct((3, count, HS), jnp.float32)] * 3,
        compiler_params=params(16),
        cost_estimate=cost(0, count),
        name="attend_own",
    )(own)


def attend_mate(split, mate, state):
    count = split.shape[1]
    first = 1 + len(mate)
    return pl.pallas_call(
        mate_kernel,
        in_specs=[VMEM] * (first + 3),
        out_specs=[VMEM] * 3,
        out_shape=[jax.ShapeDtypeStruct(x.shape, x.dtype) for x in state],
        input_output_aliases={first: 0, first + 1: 1, first + 2: 2},
        compiler_params=params(16),
        cost_estimate=cost(0, count),
        name="attend_mate",
    )(split, *mate, *state)


def attend_far(position, split, direct, plain, carried, state, groups, column, length):
    count = split.shape[1]
    return pl.pallas_call(
        functools.partial(far_kernel, column, length),
        in_specs=[SMEM] + [VMEM] * 7,
        out_specs=VMEM,
        out_shape=jax.ShapeDtypeStruct((groups, HALF, count // groups), jnp.float32),
        scratch_shapes=[pltpu.VMEM((count, HS), jnp.float32), pltpu.VMEM(plain.shape, jnp.bfloat16)],
        compiler_params=params(16),
        cost_estimate=cost(1, count),
        name="attend_far",
    )(position, split, direct, plain, carried, *state)


def summed(parts_ref):
    velocity = parts_ref[0]
    for s in range(1, parts_ref.shape[0]):
        velocity = velocity + parts_ref[s]
    return velocity


def velocity_kernel(parts_ref, velocity_ref):
    velocity_ref[...] = summed(parts_ref)


def advance_kernel(position_ref, levels_ref, timesteps_ref, parts_ref, latent_ref, fresh_ref, sent_ref):
    level = levels_ref[0]
    step = timesteps_ref[jnp.maximum(level - 2, 0)] - timesteps_ref[level]
    advanced = latent_ref[...] + (step.astype(jnp.float32) / 64.0) * summed(parts_ref)
    sent_ref[...] = jnp.where(position_ref[0] == 0, fresh_ref[...], advanced)


def advance(position, levels, timesteps, parts, latent_t, fresh_t):
    return pl.pallas_call(
        advance_kernel,
        in_specs=[SMEM] * 3 + [VMEM] * 3,
        out_specs=VMEM,
        out_shape=jax.ShapeDtypeStruct(latent_t.shape, jnp.float32),
        compiler_params=params(2),
        name="advance",
    )(position, levels, timesteps, parts, latent_t, fresh_t)


def total_velocity(parts):
    return pl.pallas_call(
        velocity_kernel,
        in_specs=[VMEM],
        out_specs=VMEM,
        out_shape=jax.ShapeDtypeStruct(parts.shape[1:], jnp.float32),
        compiler_params=params(2),
        name="velocity",
    )(parts)


def turned(pairs):
    return [(j, i) for i, j in pairs]


def on_device(queries, key_proj, values, latents, head_weight, levels, timesteps, fresh_noise):
    position = lax.axis_index("queue")[None].astype(jnp.int32)
    length = lax.axis_size("queue")
    groups = lax.axis_size("seq")
    sent = pack(position, queries[0], key_proj[0], values[0], head_weight.T, groups)
    own = lax.all_to_all(sent, "seq", split_axis=0, concat_axis=0, tiled=True)
    direct, rest, *mate = cut_rows(own, groups * CUT // 8)
    column = length // 4
    inner = [(i, i + 1) for i in range(1, length - 1, 2) if (i + 1) % column]
    cross = [(i, i + 1) for i in range(column - 1, length - 1, column)]
    along_z = [(i, i + column) for i, _ in cross] + [(j, j - column) for _, j in cross]
    along_y = [(i + column, j) for i, j in cross] + [(j - column, i) for i, j in cross]
    pairs = inner + cross
    direct = lax.ppermute(direct, "queue", pairs + turned(pairs))
    plain = lax.ppermute(rest, "queue", inner + turned(inner) + along_z)
    mates = [(i, i + 1) for i in range(0, length, 2)]
    mate = [lax.ppermute(x, "queue", mates + turned(mates)) for x in mate]
    split, *state = attend_own(own)
    state = attend_mate(split, mate, state)
    plain = passed_after(plain, split)
    carried = lax.ppermute(plain, "queue", along_y)
    parts = attend_far(position, split, direct, plain, carried, state, groups, column, length)
    parts = lax.all_to_all(parts, "seq", split_axis=0, concat_axis=0, tiled=True)
    sent = advance(position, levels, timesteps, parts, latents[0].T, fresh_noise.T)
    shifted = lax.ppermute(sent, "queue", [(i, (i - 1) % length) for i in range(length)])
    return (shifted.T[None], total_velocity(parts).T[None])


def solution(mesh):
    in_specs = (
        P("queue", "seq", None),
        P("queue", "seq", None),
        P("queue", "seq", None),
        P("queue", "seq", None),
        P(),
        P("queue"),
        P(),
        P("seq", None),
    )
    out_specs = (P("queue", "seq", None), P("queue", "seq", None))
    return jax.shard_map(
        on_device, mesh=mesh, in_specs=in_specs, out_specs=out_specs, check_vma=False
    )
```
